32 devices in a mesh: groups: 2 (over x), gx: 16 (over z, y, core).
Axes of the slice: x: 2, y: 2, z: 4, core: 2. Of those that a mesh axis runs over, the one named last changes fastest.
Arguments:
- tokens: bfloat16 [1024, 16384], P('groups', 'gx'), parts along dimension 0, as said below
- gain: float32 [16384], P('gx'), may hold values from 0.1 to 1.9
- gate_weight: bfloat16 [16384, 1664], P(None, 'gx'), may hold values from -0.046875 to 0.046875
- up_weight: bfloat16 [16384, 1664], P(None, 'gx'), may hold values from -0.046875 to 0.046875
- down_weight: bfloat16 [1664, 16384], P('gx'), may hold values from -0.21875 to 0.21875
Outputs:
- mixed: bfloat16 [1024, 16384], P('groups', 'gx'), parts along dimension 0
The draws below stay inside these ranges and needn't reach their ends.
There are 2 independent parts, one for each index of `groups`. The reference program is written for one: setup_inputs(seed, part) draws one part's arguments, and reference() takes and returns one part's arrays. A program takes and returns all parts, laid end to end along the dimension named above; an argument that names none is the same for every part. Nothing has to cross between parts.
Inputs may be any that keep to these rules, and one draw needn't show every extreme that they name: `tokens`: activations of one span.
All inputs are finite; a program needn't handle non-finite values.
Results may differ from the reference program's by a relative error of at most 0.02.
Values may be sent and summed in bfloat16 or wider, within the bound.
No kernel may reach another device: no remote copies, remote signals or barrier semaphores. Data moves between devices by JAX's collectives and lax.ppermute only.
A program may use at most 128 MiB of HBM per device.

```python
import math
import jax
import jax.numpy as jnp
from jax import lax

D = 16384
TOK = 512
FFB = 1664


def draw_tokens(key, part):
    key = jax.random.fold_in(key, 11)
    key_base, key_rows, key_cols = jax.random.split(key, 3)
    row_scale = jnp.exp(jax.random.uniform(key_rows, (TOK, 1), minval=0.0, maxval=math.log(10.0)))
    col_scale = jnp.exp(jax.random.uniform(key_cols, (1, D), minval=0.0, maxval=math.log(10.0)))
    ramp = 1.0 + 2.0 * jnp.arange(D, dtype=jnp.float32)[None, :] / (D - 1)
    base = jax.random.normal(key_base, (TOK, D))
    return (0.15 * base * row_scale * col_scale * ramp).astype(jnp.bfloat16)


def strengthened(result, key, source, target, blocks, factor):
    owner, partner = [(jnp.arange(result.shape[axis_at]) // (result.shape[axis_at] // blocks)).reshape([-1 if axis == axis_at else 1 for axis in range(result.ndim)]) for axis_at in (source, target)]
    chosen = jax.random.permutation(key, blocks)[partner]
    strong = (owner == chosen) | (owner == (partner + blocks // 2) % blocks)
    return jnp.where(strong, factor * result, result)


def levels(key, extent, pieces, low, top_value):
    level, own = 1.0, jax.random.fold_in(key, 6)
    for axis_at, shards_of in pieces:
        draws = jnp.exp(jax.random.uniform(jax.random.fold_in(own, axis_at), (shards_of,), jnp.float32, low / len(pieces), top_value / len(pieces)))
        level = level * jnp.repeat(draws, extent[axis_at] // shards_of).reshape([-1 if axis == axis_at else 1 for axis in range(len(extent))])
    return level


def bell_draw(stream_key, shape, deviation, reach, pieces=(), kind=jnp.bfloat16):
    drawn = jax.random.normal(stream_key, shape, jnp.float32) * deviation
    if len(pieces) > 0:
        drawn = levels(stream_key, shape, pieces, -0.22, 0.18) * drawn
    return jnp.clip(drawn, min=-reach, max=reach).astype(kind)


def gaussian_with(rng, shape, deviation, reach, shards, heavy, kind=jnp.bfloat16):
    values = deviation * jax.random.normal(rng, shape, jnp.float32)
    if shards:
        values = values * levels(rng, shape, shards, -0.22, 0.18)
    return jnp.clip(strengthened(values, jax.random.fold_in(rng, 3), *heavy), -reach, reach).astype(kind)


def setup_inputs(seed: int = 0, part: int = 0) -> dict:
    seeds = jax.random.split(jax.random.key(seed), 6)
    part_keys = jax.random.split(jax.random.fold_in(seeds[5], part), 6)
    tokens = draw_tokens(jax.random.fold_in(jax.random.fold_in(seeds[5], part), 71), part)
    gain = jnp.clip(1.0 + 0.18 * jax.random.normal(seeds[1], (D,), jnp.float32), 0.1, 1.9)
    gate_weight = bell_draw(seeds[2], (D, FFB), D ** -0.5, 0.046875, ((1, 16),))
    up_weight = bell_draw(seeds[3], (D, FFB), D ** -0.5, 0.046875, ((1, 16),))
    down_weight = gaussian_with(seeds[4], (FFB, D), FFB ** -0.5, 0.21875, ((0, 16),), (0, 1, 16, 2.0))
    return {"tokens": tokens, "gain": gain, "gate_weight": gate_weight, "up_weight": up_weight, "down_weight": down_weight}


def reference(tokens, gain, gate_weight, up_weight, down_weight):
    values = tokens.astype(jnp.float32)
    inverse = lax.rsqrt(lax.optimization_barrier(jnp.mean(values * values, axis=1, keepdims=True)) + 1e-05)
    scaled = (values * gain[None, :]).astype(jnp.bfloat16)
    gate = jnp.dot(scaled, gate_weight, preferred_element_type=jnp.float32) * inverse
    upper = jnp.dot(scaled, up_weight, preferred_element_type=jnp.float32) * inverse
    hidden = (jax.nn.silu(gate) * upper).astype(jnp.bfloat16)
    return jnp.dot(hidden, down_weight, preferred_element_type=jnp.float32).astype(jnp.bfloat16)
```

```python
import jax
import jax.numpy as jnp
from jax import lax
from jax.sharding import PartitionSpec as P

D = 16384
CHUNKS = 2
BF = jnp.bfloat16
F32 = jnp.float32


def make_body(n, groups):
    planes = n // 4

    def at(p, q):
        return (p % planes) * 4 + q

    def flip(d):
        return [(at(p, q), at(p, q ^ d)) for p in range(planes) for q in range(4)]

    def shift(k, d=0):
        return [(at(p, q), at(p + k, q ^ d)) for p in range(planes) for q in range(4)]

    def body(tokens, gain, gate_weight, up_weight, down_weight):
        me = lax.axis_index("gx")
        plane, quad = me // 4, me % 4
        group = lax.axis_index("groups")
        rows, width = tokens.shape
        hid = gate_weight.shape[1]
        part = width // groups

        values = tokens.astype(F32)
        squares = jnp.sum(values * values, axis=1)
        scaled = (values * gain[None, :]).astype(BF)
        total = jnp.sum(lax.all_gather(squares, "gx"), axis=0)

        both = [w.T.reshape(hid, planes, 4, width) for w in (gate_weight, up_weight)]

        def features(d):
            return jnp.stack(
                [
                    jnp.concatenate(
                        [
                            lax.dynamic_slice(w, (0, (plane + planes - s) % planes, quad ^ d, 0), (hid, 1, 1, width)).reshape(hid, width)
                            for w in both
                        ],
                        axis=0,
                    )
                    for s in range(planes)
                ]
            )

        weights = [features(0)] + [lax.ppermute(features(d), "gx", flip(d)) for d in (1, 2, 3)]

        step = rows // CHUNKS
        current = [scaled[t * step : (t + 1) * step] for t in range(CHUNKS)]
        sums = [[None] * 4 for _ in range(CHUNKS)]
        for s in range(planes):
            for t in range(CHUNKS):
                if s:
                    current[t] = lax.ppermute(current[t], "gx", shift(1))
                for d in range(4):
                    term = lax.dot_general(weights[d][s], current[t], (((1,), (1,)), ((), ())), preferred_element_type=F32)
                    sums[t][d] = term if s == 0 else sums[t][d] + term

        down = down_weight.reshape(hid, planes, 2, 2, groups, part)
        y, c = quad // 2, quad % 2

        def columns(other):
            taken = lax.dynamic_slice(down, (0, 0, 0, c ^ other, group, 0), (hid, planes, 2, 1, 1, part))
            return taken.reshape(hid, planes, 2, part).transpose(1, 2, 0, 3)

        pair = jnp.stack([columns(0), lax.ppermute(columns(1), "gx", flip(1))], axis=2)

        def side(other):
            return lax.dynamic_slice(pair, (0, y ^ other, 0, 0, 0), (planes, 1, 2, hid, part)).reshape(planes, 2, hid, part)

        four = jnp.stack([side(0), lax.ppermute(side(1), "gx", flip(2))], axis=1)
        held = []
        for k in range(planes):
            block = lax.dynamic_index_in_dim(four, (plane + planes - k) % planes, 0, keepdims=False)
            held.append(lax.ppermute(block, "gx", shift(-k)) if k else block)
        held = jnp.stack(held)
        pieces = [held] + [
            lax.ppermute(held, "groups", [((g + r) % groups, g) for g in range(groups)]) for r in range(1, groups)
        ]

        inverse = lax.rsqrt(total / D + 1e-05)[None, :]
        hidden = []
        for t in range(CHUNKS):
            own, near, across, far = sums[t]
            sent = lax.ppermute(jnp.concatenate([near, far], axis=0).astype(BF), "gx", flip(1)).astype(F32)
            own, across = own + sent[: 2 * hid], across + sent[2 * hid :]
            own = own + lax.ppermute(across.astype(BF), "gx", flip(2)).astype(F32)
            scale = inverse[:, t * step : (t + 1) * step]
            gate, up = own[:hid] * scale, own[hid:] * scale
            hidden.append((jax.nn.silu(gate) * up).astype(BF))
        hidden = jnp.concatenate(hidden, axis=1)
        near = []
        for k in range(planes):
            for d in (0, 2):
                near.append(lax.ppermute(hidden, "gx", shift(-k, d)) if k or d else hidden)
        near = jnp.stack(near).reshape(planes, 2, hid, rows)
        far = lax.ppermute(near, "gx", flip(1))
        every = jnp.stack([near, far], axis=2).reshape(n * hid, rows)

        out = jnp.zeros((rows, width), BF)
        for r in range(groups):
            mixed = lax.dot_general(
                every, pieces[r].reshape(n * hid, part), (((0,), (0,)), ((), ())), preferred_element_type=F32
            ).astype(BF)
            out = lax.dynamic_update_slice(out, mixed, (0, (group + r) % groups * part))
        return out

    return body


def solution(mesh):
    body = make_body(mesh.shape["gx"], mesh.shape["groups"])
    in_specs = (P("groups", "gx"), P("gx"), P(None, "gx"), P(None, "gx"), P("gx", None))
    out_specs = P("groups", "gx")
    return jax.shard_map(body, mesh=mesh, in_specs=in_specs, out_specs=out_specs, check_vma=False)
```

```python
import functools

import jax
import jax.numpy as jnp
from jax import lax
from jax.experimental import pallas as pl
from jax.experimental.pallas import tpu as pltpu
from jax.sharding import PartitionSpec as P

D = 16384
BF = jnp.bfloat16
F32 = jnp.float32
ANY = pl.BlockSpec(memory_space=pl.ANY)
VMEM = pl.BlockSpec(memory_space=pltpu.VMEM)
PARAMS = pltpu.CompilerParams(vmem_limit_bytes=48 * 1024 * 1024)
HEAVY = 1
EXTRA = 16


def shape(*dims, dtype=BF):
    return jax.ShapeDtypeStruct(dims, dtype)


def cost(size, flops=0):
    return pl.CostEstimate(flops=HEAVY * flops, bytes_accessed=HEAVY * size, transcendentals=0)


def move(moves, outs, *operands, after=()):
    def kernel(*refs):
        for source, where, target, there in moves(refs[: len(operands)], refs[len(operands) + len(after) :]):
            target[there] = source[where]

    return pl.pallas_call(
        kernel,
        out_shape=outs,
        in_specs=[VMEM] * len(operands) + [ANY] * len(after),
        out_specs=[VMEM] * len(outs),
        compiler_params=PARAMS,
        cost_estimate=cost(4 * sum(o.size for o in outs)),
    )(*operands, *after)


def split(values):
    parts = []
    for _ in range(3):
        parts.append(lax.reduce_precision(values, 8, 7))
        values = values - parts[-1]
    return jnp.pad(jnp.concatenate(parts), ((0, EXTRA - 3), (0, 0))).astype(BF)


def joined(parts):
    parts = parts.astype(F32)
    return parts[0:1] + parts[1:2] + parts[2:3]


def stage(kernel, outs, *operands, after=()):
    def body(*refs):
        kernel(*refs[: len(operands)], *refs[len(operands) + len(after) :])

    return pl.pallas_call(
        body,
        out_shape=outs,
        in_specs=[VMEM] * len(operands) + [ANY] * len(after),
        out_specs=[VMEM] * len(outs),
        compiler_params=PARAMS,
        cost_estimate=cost(4 * sum(o.size for o in outs)),
    )(*operands, *after)


def put_parts(values, out):
    parts = []
    for _ in range(3):
        parts.append(values.astype(BF).astype(F32))
        values = values - parts[-1]
    out[pl.ds(0, EXTRA), :] = jnp.concatenate(parts + [jnp.zeros((EXTRA - 3, values.shape[1]), F32)]).astype(BF)


def leave(sums, total, send):
    count = sums.shape[0] // 4
    put_parts(total[...], send)
    for i, d in enumerate((1, 3)):
        send[pl.ds(EXTRA + i * count, count), :] = sums[pl.ds(d * count, count), :].astype(BF)


def meet(sums, total, came, mine, total_out, send):
    count = sums.shape[0] // 4
    both = total[...] + joined(came[pl.ds(0, EXTRA), :])
    total_out[...] = both
    mine[...] = sums[pl.ds(0, count), :] + came[pl.ds(EXTRA, count), :].astype(F32)
    put_parts(both, send)
    across = sums[pl.ds(2 * count, count), :] + came[pl.ds(EXTRA + count, count), :].astype(F32)
    send[pl.ds(EXTRA, count), :] = across.astype(BF)


def activate(mine, total, came, hidden):
    hid = hidden.shape[0]
    inverse = lax.rsqrt((total[...] + joined(came[pl.ds(0, EXTRA), :])) / D + 1e-05)
    gate = (mine[pl.ds(0, hid), :] + came[pl.ds(EXTRA, hid), :].astype(F32)) * inverse
    up = (mine[pl.ds(hid, hid), :] + came[pl.ds(EXTRA + hid, hid), :].astype(F32)) * inverse
    hidden[...] = (gate / (1.0 + jnp.exp(-gate)) * up).astype(BF)


def arrivals(planes):
    order = [0]
    for s in range(1, planes // 2 + 1):
        order += [s] if 2 * s == planes else [s, planes - s]
    return order


def make_body(n, groups):
    planes = n // 4
    order = arrivals(planes)
    cuts = [range(0, planes // 2), *[range(j, j + 1) for j in range(planes // 2, planes)]] if planes <= 4 else [range(0, planes // 2), range(planes // 2, planes)]
    paired = groups % 2 == 0

    def at(p, q):
        return (p % planes) * 4 + q

    def flip(d):
        return [(at(p, q), at(p, q ^ d)) for p in range(planes) for q in range(4)]

    def shift(k, d=0):
        return [(at(p, q), at(p + k, q ^ d)) for p in range(planes) for q in range(4)]

    def far_flip():
        return [(g * n + i, g * n + j) for g in range(groups) for i, j in flip(2 + g % 2)]

    def swap(r):
        return [((g + r) % groups, g) for g in range(groups)]

    def place():
        me = lax.axis_index("gx")
        return me // 4, me % 4

    def product(spot, rows, blocks, own, near, far, js, total=None, after=()):
        width = blocks[0].shape[1]
        _, two, hid, _ = near.shape
        first, count = js[0], len(js)
        given = [] if total is None else [total]

        def kernel(spot, *refs):
            sources, refs = refs[:count], refs[count:]
            own_gate, own_up, near, far0, far1 = refs[:5]
            out, xs, sems = refs[-3:]
            i = pl.program_id(0)
            copies = [
                pltpu.make_async_copy(x.at[pl.ds(0, rows)], xs.at[k], sems.at[k]) for k, x in enumerate(sources)
            ]

            @pl.when(i == 0)
            def _():
                for copy in copies:
                    copy.start()
                out[...] = refs[5][...] if given else jnp.zeros_like(out)

            for k, copy in enumerate(copies):
                pl.when(i == k)(copy.wait)

            x = xs[i]
            weights = [own_gate[...], own_up[...]] + [w[0, j] for w in (near, far0, far1) for j in range(2)]
            for b, block in enumerate(weights):
                term = lax.dot_general(block, x, (((1,), (1,)), ((), ())), preferred_element_type=F32)
                d = b // 2 if b < 4 else 2 + lax.bitwise_xor(b // 2 - 2, spot[2])
                out[pl.ds(pl.multiple_of((d * 2 + b % 2) * hid, 8), hid), :] += term

        near_block = pl.BlockSpec((1, two, hid, width), lambda i, spot: (i + first, 0, 0, 0))
        far_block = pl.BlockSpec((1, two, hid, width), lambda i, spot: (i, 0, 0, 0))
        mine = pl.BlockSpec((hid, width), lambda i, spot: (0, spot[3 + first + i] * 4 + spot[1]))
        whole = pl.BlockSpec((8 * hid, rows), lambda i, spot: (0, 0))
        return pl.pallas_call(
            kernel,
            grid_spec=pltpu.PrefetchScalarGridSpec(
                num_scalar_prefetch=1,
                grid=(count,),
                in_specs=[ANY] * count
                + [mine, mine, near_block, far_block, far_block]
                + [whole] * len(given)
                + [ANY] * len(after),
                out_specs=whole,
                scratch_shapes=[pltpu.VMEM((count, rows, width), BF), pltpu.SemaphoreType.DMA((count,))],
            ),
            out_shape=shape(8 * hid, rows, dtype=F32),
            compiler_params=PARAMS,
            cost_estimate=cost(16 * hid * width * count, 16 * hid * rows * width * count),
        )(spot, *[blocks[j] for j in js], *own, near, *far, *given, *after)

    def cut(spot, gate_t, up_t, width, ds, first, count, after=()):
        hid = gate_t.shape[0]

        def kernel(spot, *refs):
            outs = refs[2 * len(ds) + len(after) :]
            for d, out in enumerate(outs):
                for j in range(2):
                    out[0, j] = refs[2 * d + j][...]

        def taken(d):
            def index(s, spot):
                other = lax.bitwise_xor(spot[1], d + spot[2] if d == 2 and paired else d)
                return 0, spot[3 + first + s] * 4 + other

            return pl.BlockSpec((hid, width), index)

        return pl.pallas_call(
            kernel,
            grid_spec=pltpu.PrefetchScalarGridSpec(
                num_scalar_prefetch=1,
                grid=(count,),
                in_specs=[taken(d) for d in ds for _ in range(2)] + [ANY] * len(after),
                out_specs=[pl.BlockSpec((1, 2, hid, width), lambda s, spot: (s, 0, 0, 0))] * len(ds),
            ),
            out_shape=[shape(count, 2, hid, width)] * len(ds),
            compiler_params=PARAMS,
            cost_estimate=cost(8 * len(ds) * count * hid * width),
        )(spot, *[gate_t, up_t] * len(ds), *after)

    def mix(side, pieces, share, dc, total=None):
        rows = side.shape[-1]
        part = pieces[0].shape[-1]
        hid = side.shape[2]
        given = [] if total is None else [total]

        def kernel(side, *refs):
            out = refs[-1]
            g = lax.axis_index("groups")
            for r in range(share):
                sums = refs[-2][r] if given else None
                for k in range(planes):
                    for dy in range(2):
                        term = lax.dot_general(
                            side[k, dy],
                            refs[r * planes + k][dy, dc],
                            (((0,), (0,)), ((), ())),
                            preferred_element_type=F32,
                        )
                        sums = term if sums is None else sums + term
                if not given:
                    out[r] = sums
                elif share == 1:
                    out[...] = sums.astype(BF)
                else:
                    out[:, pl.ds(pl.multiple_of((g + r) % share * part, part), part)] = sums.astype(BF)

        return pl.pallas_call(
            kernel,
            out_shape=shape(rows, share * part) if given else shape(share, rows, part, dtype=F32),
            in_specs=[VMEM] * (1 + len(pieces) + len(given)),
            out_specs=VMEM,
            compiler_params=PARAMS,
            cost_estimate=cost(n * hid * (rows + share * part), rows * n * hid * share * part),
        )(side, *pieces, *given)

    def body(tokens, gain, gate_weight, up_weight, down_weight):
        rows, width = tokens.shape
        hid = gate_weight.shape[1]
        share = groups if width // groups % 128 == 0 else 1
        part = width // share
        own = gate_weight.T, up_weight.T
        me = lax.axis_index("gx")
        plane, quad = me // 4, me % 4
        half = lax.axis_index("groups") % 2 if paired else jnp.int32(0)
        spot = jnp.stack([plane, quad, half] + [lax.rem(plane + planes - s, planes) for s in order])

        values = tokens.astype(F32)
        squares = split(jnp.sum(values * values, axis=1)[None, :])
        lanes = min(rows, width)
        extra = jnp.concatenate([squares[:, i : i + lanes] for i in range(0, rows, lanes)])
        scaled = (values * gain[None, :]).astype(BF)
        blocks = [jnp.concatenate([scaled, jnp.pad(extra, ((0, 0), (0, width - lanes)))])]
        for s in order[1:]:
            way = 1 if 2 * s <= planes else -1
            last = blocks[0] if len(blocks) < 3 else blocks[-2]
            blocks.append(lax.ppermute(last, "gx", shift(way)))
        parts = [b[rows + i : rows + i + EXTRA, :lanes] for b in blocks for i in range(0, len(extra), EXTRA)]
        parts = [jnp.concatenate([joined(p) for p in parts[i :: len(extra) // EXTRA]]) for i in range(len(extra) // EXTRA)]
        total = jnp.concatenate([jnp.sum(p, axis=0, keepdims=True) for p in parts], axis=1)

        def first_moves(given, outs):
            _, quad = place()
            g = lax.axis_index("groups") if share > 1 else 0
            moves = []
            for other in range(2):
                for p in range(planes):
                    for y in range(2):
                        target = p * 4 + y * 2 + lax.bitwise_xor(lax.rem(quad, 2), other)
                        columns = pl.ds(pl.multiple_of(target * width + g * part, part), part)
                        moves.append((given[0], (slice(None), columns), outs[other], (y, p)))
            return moves

        keep, send = move(first_moves, [shape(2, planes, hid, part)] * 2, down_weight)
        came = lax.ppermute(send, "gx", flip(1))

        def second_moves(given, outs):
            _, quad = place()
            return [(given[dc], lax.bitwise_xor(quad // 2, 1), outs[0], dc) for dc in range(2)]

        send = move(second_moves, [shape(2, planes, hid, part)], keep, came)[0]
        across = lax.ppermute(send, "gx", flip(2))

        def third_moves(given, outs):
            plane, quad = place()
            moves = []
            for k in range(planes):
                p = lax.rem(plane + planes - k, planes)
                for dc in range(2):
                    moves.append((given[dc], (quad // 2, p), outs[k], (0, dc)))
                    moves.append((given[2], (dc, p), outs[k], (1, dc)))
            return moves

        ready = move(third_moves, [shape(2, 2, hid, part)] * planes, keep, came, across)
        held = [lax.ppermute(h, "gx", shift(-k)) if k else h for k, h in enumerate(ready)]
        pieces = list(held)
        for r in range(1, share):
            pieces += [lax.ppermute(h, "groups", swap(r)) for h in held]

        far = []
        for i, js in enumerate(cuts):
            sends = cut(spot, *own, width, (2,) if paired else (2, 3), js[0], len(js), after=(send,) if i else ())
            if paired:
                came = lax.ppermute(sends[0], ("groups", "gx"), far_flip())
                far.append((came, lax.ppermute(came, "groups", [(i, i ^ 1) for i in range(groups)])))
            else:
                far.append(tuple(lax.ppermute(w, "gx", flip(d)) for d, w in zip((2, 3), sends)))
        near = lax.ppermute(cut(spot, *own, width, (1,), 0, planes)[0], "gx", flip(1))

        sums = None
        crossed = pieces[planes:] if share > 1 else held
        needs = [(ready[0],), (held[1],), (held[-1], crossed[0])]
        later = [(crossed[1],), (crossed[-1], held[2 % planes])]
        for i, js in enumerate(cuts):
            sums = product(spot, rows, blocks, own, near, far[i], js, sums, after=needs[i])

        send = stage(leave, [shape(EXTRA + 4 * hid, rows)], sums, total)[0]
        came = lax.ppermute(send, "gx", flip(1))
        mine, total, send = stage(
            meet, [shape(2 * hid, rows, dtype=F32), shape(1, rows, dtype=F32), shape(EXTRA + 2 * hid, rows)], sums, total, came,
            after=later[0],
        )
        came = lax.ppermute(send, "gx", flip(2))
        hidden = stage(activate, [shape(hid, rows)], mine, total, came, after=later[1])[0]
        beside = [lax.ppermute(hidden, "gx", shift(-k, d)) if k or d else hidden for k in range(planes) for d in (0, 2)]
        beside = move(
            lambda given, outs: [(a, ..., outs[0], (i // 2, i % 2)) for i, a in enumerate(given)],
            [shape(planes, 2, hid, rows)],
            *beside,
        )[0]
        other = lax.ppermute(beside, "gx", flip(1))
        return mix(other, pieces, share, 1, mix(beside, pieces, share, 0))

    return body


def solution(mesh):
    body = make_body(mesh.shape["gx"], mesh.shape["groups"])
    in_specs = (P("groups", "gx"), P("gx"), P(None, "gx"), P(None, "gx"), P("gx", None))
    out_specs = P("groups", "gx")
    return jax.shard_map(body, mesh=mesh, in_specs=in_specs, out_specs=out_specs, check_vma=False)
```

```python
import functools

import jax
import jax.numpy as jnp
from jax import lax
from jax.experimental import pallas as pl
from jax.experimental.pallas import tpu as pltpu
from jax.sharding import PartitionSpec as P

D = 16384
BF = jnp.bfloat16
F32 = jnp.float32
ANY = pl.BlockSpec(memory_space=pl.ANY)
VMEM = pl.BlockSpec(memory_space=pltpu.VMEM)
PARAMS = pltpu.CompilerParams(vmem_limit_bytes=48 * 1024 * 1024)
HEAVY = 20
EXTRA = 16


def shape(*dims, dtype=BF):
    return jax.ShapeDtypeStruct(dims, dtype)


def cost(size, flops=0, heavy=HEAVY):
    return pl.CostEstimate(flops=int(heavy * flops), bytes_accessed=int(heavy * size), transcendentals=0)


def move(moves, outs, *operands, after=()):
    def kernel(*refs):
        for source, where, target, there in moves(refs[: len(operands)], refs[len(operands) + len(after) :]):
            target[there] = source[where]

    return pl.pallas_call(
        kernel,
        out_shape=outs,
        in_specs=[VMEM] * len(operands) + [ANY] * len(after),
        out_specs=[VMEM] * len(outs),
        compiler_params=PARAMS,
        cost_estimate=cost(4 * sum(o.size for o in outs), 0, 20),
    )(*operands, *after)


def split(values):
    parts = []
    for _ in range(3):
        parts.append(lax.reduce_precision(values, 8, 7))
        values = values - parts[-1]
    return jnp.pad(jnp.concatenate(parts), ((0, EXTRA - 3), (0, 0))).astype(BF)


def joined(parts):
    parts = parts.astype(F32)
    return parts[0:1] + parts[1:2] + parts[2:3]


def stage(kernel, outs, *operands, after=()):
    def body(*refs):
        kernel(*refs[: len(operands)], *refs[len(operands) + len(after) :])

    return pl.pallas_call(
        body,
        out_shape=outs,
        in_specs=[VMEM] * len(operands) + [ANY] * len(after),
        out_specs=[VMEM] * len(outs),
        compiler_params=PARAMS,
        cost_estimate=cost(4 * sum(o.size for o in outs), 0, 0),
    )(*operands, *after)


def put_parts(values, out):
    parts = []
    for _ in range(3):
        parts.append(values.astype(BF).astype(F32))
        values = values - parts[-1]
    out[pl.ds(0, EXTRA), :] = jnp.concatenate(parts + [jnp.zeros((EXTRA - 3, values.shape[1]), F32)]).astype(BF)


def leave(sums, total, send):
    count = sums.shape[0] // 4
    put_parts(total[...], send)
    for i, d in enumerate((1, 3)):
        send[pl.ds(EXTRA + i * count, count), :] = sums[pl.ds(d * count, count), :].astype(BF)


def meet(sums, total, came, mine, total_out, send):
    count = sums.shape[0] // 4
    both = total[...] + joined(came[pl.ds(0, EXTRA), :])
    total_out[...] = both
    mine[...] = sums[pl.ds(0, count), :] + came[pl.ds(EXTRA, count), :].astype(F32)
    put_parts(both, send)
    across = sums[pl.ds(2 * count, count), :] + came[pl.ds(EXTRA + count, count), :].astype(F32)
    send[pl.ds(EXTRA, count), :] = across.astype(BF)


def activate(mine, total, came, hidden):
    hid = hidden.shape[0]
    inverse = lax.rsqrt((total[...] + joined(came[pl.ds(0, EXTRA), :])) / D + 1e-05)
    gate = (mine[pl.ds(0, hid), :] + came[pl.ds(EXTRA, hid), :].astype(F32)) * inverse
    up = (mine[pl.ds(hid, hid), :] + came[pl.ds(EXTRA + hid, hid), :].astype(F32)) * inverse
    hidden[...] = (gate / (1.0 + jnp.exp(-gate)) * up).astype(BF)


def arrivals(planes):
    table = []
    for p in range(planes):
        row = [(0, p)]
        for s in range(1, planes):
            if p >= s:
                row.append((2 * s - 1, p - s))
            if p + s < planes:
                row.append((2 * s, p + s))
        table.append(row)
    return table


def make_body(n, groups):
    planes = n // 4
    table = arrivals(planes)
    BLOCK, ARRAY = 3, 3 + planes
    cuts = [range(0, planes // 2), range(planes // 2, planes)]
    paired = groups % 2 == 0

    def at(p, q):
        return (p % planes) * 4 + q

    def flip(d):
        return [(at(p, q), at(p, q ^ d)) for p in range(planes) for q in range(4)]

    def shift(k, d=0):
        return [(at(p, q), at(p + k, q ^ d)) for p in range(planes) for q in range(4)]

    def line(s, way):
        senders = range(s - 1, planes - 1) if way > 0 else range(1, planes - s + 1)
        return [(at(p, q), at(p + way, q)) for p in senders for q in range(4)]

    def far_flip():
        return [(g * n + i, g * n + j) for g in range(groups) for i, j in flip(2 + g % 2)]

    def swap(r):
        return [((g + r) % groups, g) for g in range(groups)]

    def place():
        me = lax.axis_index("gx")
        return me // 4, me % 4

    def product(spot, rows, blocks, own, near, far, js, total=None, after=()):
        width = blocks[0].shape[1]
        _, two, hid, _ = near.shape
        first, count = js[0], len(js)
        lists = [sorted(set(row[j][0] for row in table)) for j in js]
        arrays = sorted(set(sum(lists, [])))
        given = [] if total is None else [total]

        def kernel(spot, *refs):
            sources, refs = refs[: len(arrays)], refs[len(arrays) :]
            own_gate, own_up, near, far0, far1 = refs[:5]
            out, xs, sems = refs[-3:]
            i = pl.program_id(0)

            def bring(array, k):
                return pltpu.make_async_copy(sources[arrays.index(array)].at[pl.ds(0, rows)], xs.at[k], sems.at[k])

            @pl.when(i == 0)
            def _():
                for k, choices in enumerate(lists):
                    for array in choices:
                        pl.when(spot[ARRAY + first + k] == array)(bring(array, k).start)
                out[...] = refs[5][...] if given else jnp.zeros_like(out)

            for k, choices in enumerate(lists):
                pl.when(i == k)(bring(choices[0], k).wait)

            x = xs[i]
            weights = [own_gate[...], own_up[...]] + [w[0, j] for w in (near, far0, far1) for j in range(2)]
            term = lax.dot_general(
                jnp.concatenate(weights), x, (((1,), (1,)), ((), ())), preferred_element_type=F32
            )
            out[pl.ds(0, 4 * hid), :] += term[: 4 * hid]
            for b in range(2):
                d = 2 + lax.bitwise_xor(b, spot[2])
                out[pl.ds(pl.multiple_of(d * 2 * hid, 8), 2 * hid), :] += term[(4 + 2 * b) * hid : (6 + 2 * b) * hid]

        near_block = pl.BlockSpec((1, two, hid, width), lambda i, spot: (i + first, 0, 0, 0))
        far_block = pl.BlockSpec((1, two, hid, width), lambda i, spot: (i, 0, 0, 0))
        mine = pl.BlockSpec((hid, width), lambda i, spot: (0, spot[BLOCK + first + i] * 4 + spot[1]))
        whole = pl.BlockSpec((8 * hid, rows), lambda i, spot: (0, 0))
        return pl.pallas_call(
            kernel,
            grid_spec=pltpu.PrefetchScalarGridSpec(
                num_scalar_prefetch=1,
                grid=(count,),
                in_specs=[ANY] * len(arrays)
                + [mine, mine, near_block, far_block, far_block]
                + [whole] * len(given)
                + [ANY] * len(after),
                out_specs=whole,
                scratch_shapes=[pltpu.VMEM((count, rows, width), BF), pltpu.SemaphoreType.DMA((count,))],
            ),
            out_shape=shape(8 * hid, rows, dtype=F32),
            compiler_params=PARAMS,
            cost_estimate=cost(16 * hid * width * count, 16 * hid * rows * width * count, 1),
        )(spot, *[blocks[m] for m in arrays], *own, near, *far, *given, *after)

    def cut(spot, gate_t, up_t, width, ds, first, count, after=()):
        hid = gate_t.shape[0]

        def kernel(spot, *refs):
            outs = refs[2 * len(ds) + len(after) :]
            for d, out in enumerate(outs):
                for j in range(2):
                    out[0, j] = refs[2 * d + j][...]

        def taken(d):
            def index(s, spot):
                other = lax.bitwise_xor(spot[1], d + spot[2] if d == 2 and paired else d)
                return 0, spot[BLOCK + first + s] * 4 + other

            return pl.BlockSpec((hid, width), index)

        return pl.pallas_call(
            kernel,
            grid_spec=pltpu.PrefetchScalarGridSpec(
                num_scalar_prefetch=1,
                grid=(count,),
                in_specs=[taken(d) for d in ds for _ in range(2)] + [ANY] * len(after),
                out_specs=[pl.BlockSpec((1, 2, hid, width), lambda s, spot: (s, 0, 0, 0))] * len(ds),
            ),
            out_shape=[shape(count, 2, hid, width)] * len(ds),
            compiler_params=PARAMS,
            cost_estimate=cost(8 * len(ds) * count * hid * width, 0, 20),
        )(spot, *[gate_t, up_t] * len(ds), *after)

    def mix(side, pieces, share, dc, total=None):
        rows = side.shape[-1]
        part = pieces[0].shape[-1]
        hid = side.shape[2]
        given = [] if total is None else [total]

        def kernel(side, *refs):
            out = refs[-1]
            g = lax.axis_index("groups")
            left = jnp.concatenate([side[k, dy] for k in range(planes) for dy in range(2)])
            for r in range(share):
                held = refs[r * planes : (r + 1) * planes]
                right = jnp.concatenate([h[dy, 0] for h in held for dy in range(2)])
                sums = lax.dot_general(left, right, (((0,), (0,)), ((), ())), preferred_element_type=F32)
                if not given:
                    out[r] = sums
                    continue
                sums = (refs[-2][r] + sums).astype(BF)
                if share == 1:
                    out[...] = sums
                else:
                    out[:, pl.ds(pl.multiple_of((g + r) % share * part, part), part)] = sums

        half = pl.BlockSpec((2, 1, hid, part), lambda i: (0, dc, 0, 0))
        full = [pl.BlockSpec(a.shape, functools.partial(lambda n, i: (0,) * n, a.ndim)) for a in (side, *given)]
        out_shape = (rows, share * part) if given else (share, rows, part)
        return pl.pallas_call(
            kernel,
            grid=(1,),
            out_shape=shape(*out_shape, dtype=BF if given else F32),
            in_specs=full[:1] + [half] * len(pieces) + full[1:],
            out_specs=pl.BlockSpec(out_shape, lambda i: (0,) * len(out_shape)),
            compiler_params=PARAMS,
            cost_estimate=cost(n * hid * (rows + share * part), rows * n * hid * share * part),
        )(side, *pieces, *given)

    def body(tokens, gain, gate_weight, up_weight, down_weight):
        rows, width = tokens.shape
        hid = gate_weight.shape[1]
        share = groups if width // groups % 128 == 0 else 1
        part = width // share
        own = gate_weight.T, up_weight.T
        me = lax.axis_index("gx")
        plane, quad = me // 4, me % 4
        half = lax.axis_index("groups") % 2 if paired else jnp.int32(0)
        turns = jnp.array([[p for _, p in row] + [m for m, _ in row] for row in table], jnp.int32)
        spot = jnp.concatenate([jnp.stack([plane, quad, half]), lax.dynamic_index_in_dim(turns, plane, 0, keepdims=False)])

        values = tokens.astype(F32)
        squares = split(jnp.sum(values * values, axis=1)[None, :])
        lanes = min(rows, width)
        extra = jnp.concatenate([squares[:, i : i + lanes] for i in range(0, rows, lanes)])
        scaled = (values * gain[None, :]).astype(BF)
        blocks = [jnp.concatenate([scaled, jnp.pad(extra, ((0, 0), (0, width - lanes)))])]
        for s in range(1, planes):
            for way in (1, -1):
                blocks.append(lax.ppermute(blocks[0] if s == 1 else blocks[-2], "gx", line(s, way)))
        parts = [b[rows + i : rows + i + EXTRA, :lanes] for b in blocks for i in range(0, len(extra), EXTRA)]
        parts = [jnp.concatenate([joined(p) for p in parts[i :: len(extra) // EXTRA]]) for i in range(len(extra) // EXTRA)]
        total = jnp.concatenate([jnp.sum(p, axis=0, keepdims=True) for p in parts], axis=1)

        def first_moves(given, outs):
            _, quad = place()
            g = lax.axis_index("groups") if share > 1 else 0
            moves = []
            for other in range(2):
                for p in range(planes):
                    for y in range(2):
                        target = p * 4 + y * 2 + lax.bitwise_xor(lax.rem(quad, 2), other)
                        columns = pl.ds(pl.multiple_of(target * width + g * part, part), part)
                        moves.append((given[0], (slice(None), columns), outs[other], (y, p)))
            return moves

        keep, send = move(first_moves, [shape(2, planes, hid, part)] * 2, down_weight)
        came = lax.ppermute(send, "gx", flip(1))

        def second_moves(given, outs):
            _, quad = place()
            return [(given[dc], lax.bitwise_xor(quad // 2, 1), outs[0], dc) for dc in range(2)]

        send = move(second_moves, [shape(2, planes, hid, part)], keep, came, after=(blocks[0],))[0]
        across = lax.ppermute(send, "gx", flip(2))

        far = []
        for i, js in enumerate(cuts):
            sends = cut(spot, *own, width, (2,) if paired else (2, 3), js[0], len(js), after=((send,) if far else (blocks[0],)))
            if paired:
                brought = lax.ppermute(sends[0], ("groups", "gx"), far_flip())
                far.append((brought, lax.ppermute(brought, "groups", [(i, i ^ 1) for i in range(groups)])))
            else:
                far.append(tuple(lax.ppermute(w, "gx", flip(d)) for d, w in zip((2, 3), sends)))
        near = lax.ppermute(cut(spot, *own, width, (1,), 0, planes, after=(blocks[0],))[0], "gx", flip(1))

        sums = product(spot, rows, blocks, own, near, far[0], cuts[0])


        def third_moves(ks, given, outs):
            plane, quad = place()
            moves = []
            for i, k in enumerate(ks):
                p = lax.rem(plane + planes - k, planes)
                for dc in range(2):
                    moves.append((given[dc], (quad // 2, p), outs[i], (0, dc)))
                    moves.append((given[2], (dc, p), outs[i], (1, dc)))
            return moves

        ready = move(
            functools.partial(third_moves, range(planes)), [shape(2, 2, hid, part)] * planes, keep, came, across, after=(sums, *blocks[-4:-2])
        )
        held = [lax.ppermute(h, "gx", shift(-k)) if k else h for k, h in enumerate(ready)]
        pieces = list(held)
        for r in range(1, share):
            pieces += [lax.ppermute(h, "groups", swap(r)) for h in held]

        crossed = pieces[planes:] if share > 1 else held
        one, two, three = held[1], held[2 % planes], held[-1]
        x0, x1, x2, x3 = crossed[0], crossed[1], crossed[2 % planes], crossed[-1]
        later = [(two,), (one,), (three, x2)]
        sums = product(spot, rows, blocks, own, near, far[1], cuts[1], sums, after=(x0,))
        send = stage(leave, [shape(EXTRA + 4 * hid, rows)], sums, total, after=())[0]
        came = lax.ppermute(send, "gx", flip(1))
        mine, total, send = stage(
            meet, [shape(2 * hid, rows, dtype=F32), shape(1, rows, dtype=F32), shape(EXTRA + 2 * hid, rows)], sums, total, came,
            after=later[0],
        )
        came = lax.ppermute(send, "gx", flip(2))
        hidden = stage(activate, [shape(hid, rows)], mine, total, came, after=later[1])[0]
        beside = [lax.ppermute(hidden, "gx", shift(-k, d)) if k or d else hidden for k in range(planes) for d in (0, 2)]
        beside = move(
            lambda given, outs: [(a, ..., outs[0], (i // 2, i % 2)) for i, a in enumerate(given)],
            [shape(planes, 2, hid, rows)],
            *beside,
            after=later[2],
        )[0]
        other = lax.ppermute(beside, "gx", flip(1))
        return mix(other, pieces, share, 1, mix(beside, pieces, share, 0))

    return body


def solution(mesh):
    body = make_body(mesh.shape["gx"], mesh.shape["groups"])
    in_specs = (P("groups", "gx"), P("gx"), P(None, "gx"), P(None, "gx"), P("gx", None))
    out_specs = P("groups", "gx")
    return jax.shard_map(body, mesh=mesh, in_specs=in_specs, out_specs=out_specs, check_vma=False)
```

```python
import functools

import jax
import jax.numpy as jnp
from jax import lax
from jax.experimental import pallas as pl
from jax.experimental.pallas import tpu as pltpu
from jax.sharding import PartitionSpec as P

D = 16384
BF = jnp.bfloat16
F32 = jnp.float32
ANY = pl.BlockSpec(memory_space=pl.ANY)
VMEM = pl.BlockSpec(memory_space=pltpu.VMEM)
PARAMS = pltpu.CompilerParams(vmem_limit_bytes=48 * 1024 * 1024)
HEAVY = 20
EXTRA = 16


def shape(*dims, dtype=BF):
    return jax.ShapeDtypeStruct(dims, dtype)


def cost(size, flops=0, heavy=HEAVY):
    return pl.CostEstimate(flops=int(heavy * flops), bytes_accessed=int(heavy * size), transcendentals=0)


def move(moves, outs, *operands, after=()):
    def kernel(*refs):
        for source, where, target, there in moves(refs[: len(operands)], refs[len(operands) + len(after) :]):
            target[there] = source[where]

    return pl.pallas_call(
        kernel,
        out_shape=outs,
        in_specs=[VMEM] * len(operands) + [ANY] * len(after),
        out_specs=[VMEM] * len(outs),
        compiler_params=PARAMS,
        cost_estimate=cost(4 * sum(o.size for o in outs), 0, 1),
    )(*operands, *after)


def split(values):
    parts = []
    for _ in range(3):
        parts.append(lax.reduce_precision(values, 8, 7))
        values = values - parts[-1]
    return jnp.pad(jnp.concatenate(parts), ((0, EXTRA - 3), (0, 0))).astype(BF)


def joined(parts):
    parts = parts.astype(F32)
    return parts[0:1] + parts[1:2] + parts[2:3]


def stage(kernel, outs, *operands, after=()):
    def body(*refs):
        kernel(*refs[: len(operands)], *refs[len(operands) + len(after) :])

    return pl.pallas_call(
        body,
        out_shape=outs,
        in_specs=[VMEM] * len(operands) + [ANY] * len(after),
        out_specs=[VMEM] * len(outs),
        compiler_params=PARAMS,
        cost_estimate=cost(4 * sum(o.size for o in outs), 0, 1),
    )(*operands, *after)


def put_parts(values, out):
    parts = []
    for _ in range(3):
        parts.append(values.astype(BF).astype(F32))
        values = values - parts[-1]
    out[pl.ds(0, EXTRA), :] = jnp.concatenate(parts + [jnp.zeros((EXTRA - 3, values.shape[1]), F32)]).astype(BF)


def meet(keep, total, came, mine, total_out, send):
    count = keep.shape[0] // 2
    both = total[...] + joined(came[pl.ds(0, EXTRA), :])
    total_out[...] = both
    mine[...] = keep[pl.ds(0, count), :] + came[pl.ds(EXTRA, count), :].astype(F32)
    put_parts(both, send)
    across = keep[pl.ds(count, count), :] + came[pl.ds(EXTRA + count, count), :].astype(F32)
    send[pl.ds(EXTRA, count), :] = across.astype(BF)


def activate(mine, total, came, hidden):
    hid = hidden.shape[0]
    inverse = lax.rsqrt((total[...] + joined(came[pl.ds(0, EXTRA), :])) / D + 1e-05)
    gate = (mine[pl.ds(0, hid), :] + came[pl.ds(EXTRA, hid), :].astype(F32)) * inverse
    up = (mine[pl.ds(hid, hid), :] + came[pl.ds(EXTRA + hid, hid), :].astype(F32)) * inverse
    hidden[...] = (gate / (1.0 + jnp.exp(-gate)) * up).astype(BF)


def arrivals(planes):
    table = []
    for p in range(planes):
        row = [(0, p)]
        for s in range(1, planes):
            if p >= s:
                row.append((2 * s - 1, p - s))
            if p + s < planes:
                row.append((2 * s, p + s))
        table.append(row)
    return table


def make_body(n, groups):
    planes = n // 4
    table = arrivals(planes)
    BLOCK, ARRAY = 3, 3 + planes
    cuts = [range(0, planes - 1), range(planes - 1, planes)]
    paired = groups % 2 == 0

    def at(p, q):
        return (p % planes) * 4 + q

    def flip(d):
        return [(at(p, q), at(p, q ^ d)) for p in range(planes) for q in range(4)]

    def shift(k, d=0):
        return [(at(p, q), at(p + k, q ^ d)) for p in range(planes) for q in range(4)]

    def line(s, way):
        senders = range(s - 1, planes - 1) if way > 0 else range(1, planes - s + 1)
        return [(at(p, q), at(p + way, q)) for p in senders for q in range(4)]

    def far_flip():
        return [(g * n + i, g * n + j) for g in range(groups) for i, j in flip(2 + g % 2)]

    def swap(r):
        return [((g + r) % groups, g) for g in range(groups)]

    def place():
        me = lax.axis_index("gx")
        return me // 4, me % 4

    def product(spot, rows, blocks, own, near, far, js, total=None, squares=None, after=()):
        width = blocks[0].shape[1]
        _, two, hid, _ = near.shape
        first, count = js[0], len(js)
        lists = [sorted(set(row[j][0] for row in table)) for j in js]
        arrays = sorted(set(sum(lists, [])))
        last = squares is not None
        given = ([] if total is None else [total]) + ([squares] if last else [])

        def kernel(spot, *refs):
            sources, refs = refs[: len(arrays)], refs[len(arrays) :]
            own_gate, own_up, near, far0, far1 = refs[:5]
            if last:
                keep, send, out, xs, sems = refs[-5:]
            else:
                out, xs, sems = refs[-3:]
            i = pl.program_id(0)

            def bring(array, k):
                return pltpu.make_async_copy(sources[arrays.index(array)].at[pl.ds(0, rows)], xs.at[k], sems.at[k])

            @pl.when(i == 0)
            def _():
                for k, choices in enumerate(lists):
                    for array in choices:
                        pl.when(spot[ARRAY + first + k] == array)(bring(array, k).start)
                out[...] = jnp.zeros_like(out) if total is None else refs[5][...]

            for k, choices in enumerate(lists):
                pl.when(i == k)(bring(choices[0], k).wait)

            x = xs[i]
            weights = [own_gate[...], own_up[...]] + [w[0, j] for w in (near, far0, far1) for j in range(2)]
            term = lax.dot_general(
                jnp.concatenate(weights), x, (((1,), (1,)), ((), ())), preferred_element_type=F32
            )
            out[pl.ds(0, 4 * hid), :] += term[: 4 * hid]
            for b in range(2):
                d = 2 + lax.bitwise_xor(b, spot[2])
                out[pl.ds(pl.multiple_of(d * 2 * hid, 8), 2 * hid), :] += term[(4 + 2 * b) * hid : (6 + 2 * b) * hid]
            if last:

                @pl.when(i == count - 1)
                def _():
                    put_parts(refs[4 + len(given)][...], send)
                    for b in range(2):
                        keep[pl.ds(b * 2 * hid, 2 * hid), :] = out[pl.ds(b * 4 * hid, 2 * hid), :]
                        send[pl.ds(EXTRA + b * 2 * hid, 2 * hid), :] = out[pl.ds((4 * b + 2) * hid, 2 * hid), :].astype(BF)

        near_block = pl.BlockSpec((1, two, hid, width), lambda i, spot: (i + first, 0, 0, 0))
        far_block = pl.BlockSpec((1, two, hid, width), lambda i, spot: (i, 0, 0, 0))
        mine = pl.BlockSpec((hid, width), lambda i, spot: (0, spot[BLOCK + first + i] * 4 + spot[1]))

        def whole(*dims):
            return pl.BlockSpec(dims, lambda i, spot: (0, 0))

        scratch = [pltpu.VMEM((count, rows, width), BF), pltpu.SemaphoreType.DMA((count,))]
        if last:
            outs = [shape(4 * hid, rows, dtype=F32), shape(EXTRA + 4 * hid, rows)]
            scratch = [pltpu.VMEM((8 * hid, rows), F32)] + scratch
        else:
            outs = shape(8 * hid, rows, dtype=F32)
        return pl.pallas_call(
            kernel,
            grid_spec=pltpu.PrefetchScalarGridSpec(
                num_scalar_prefetch=1,
                grid=(count,),
                in_specs=[ANY] * len(arrays)
                + [mine, mine, near_block, far_block, far_block]
                + [whole(*g.shape) for g in given]
                + [ANY] * len(after),
                out_specs=[whole(*o.shape) for o in outs] if last else whole(*outs.shape),
                scratch_shapes=scratch,
            ),
            out_shape=outs,
            compiler_params=PARAMS,
            cost_estimate=cost(16 * hid * width * count, 16 * hid * rows * width * count, 1 if last else 1),
        )(spot, *[blocks[m] for m in arrays], *own, near, *far, *given, *after)

    def cut(spot, gate_t, up_t, width, ds, first, count, after=()):
        hid = gate_t.shape[0]

        def kernel(spot, *refs):
            outs = refs[2 * len(ds) + len(after) :]
            for d, out in enumerate(outs):
                for j in range(2):
                    out[0, j] = refs[2 * d + j][...]

        def taken(d):
            def index(s, spot):
                other = lax.bitwise_xor(spot[1], d + spot[2] if d == 2 and paired else d)
                return 0, spot[BLOCK + first + s] * 4 + other

            return pl.BlockSpec((hid, width), index)

        return pl.pallas_call(
            kernel,
            grid_spec=pltpu.PrefetchScalarGridSpec(
                num_scalar_prefetch=1,
                grid=(count,),
                in_specs=[taken(d) for d in ds for _ in range(2)] + [ANY] * len(after),
                out_specs=[pl.BlockSpec((1, 2, hid, width), lambda s, spot: (s, 0, 0, 0))] * len(ds),
            ),
            out_shape=[shape(count, 2, hid, width)] * len(ds),
            compiler_params=PARAMS,
            cost_estimate=cost(8 * len(ds) * count * hid * width, 0, 1),
        )(spot, *[gate_t, up_t] * len(ds), *after)

    def mix(side, pieces, share, dc, total=None):
        rows = side.shape[-1]
        part = pieces[0].shape[-1]
        hid = side.shape[2]
        given = [] if total is None else [total]

        def kernel(side, *refs):
            out = refs[-1]
            g = lax.axis_index("groups")
            left = jnp.concatenate([side[k, dy] for k in range(planes) for dy in range(2)])
            for r in range(share):
                held = refs[r * planes : (r + 1) * planes]
                right = jnp.concatenate([h[dy, 0] for h in held for dy in range(2)])
                sums = lax.dot_general(left, right, (((0,), (0,)), ((), ())), preferred_element_type=F32)
                if not given:
                    out[r] = sums
                    continue
                sums = (refs[-2][r] + sums).astype(BF)
                if share == 1:
                    out[...] = sums
                else:
                    out[:, pl.ds(pl.multiple_of((g + r) % share * part, part), part)] = sums

        half = pl.BlockSpec((2, 1, hid, part), lambda i: (0, dc, 0, 0))
        full = [pl.BlockSpec(a.shape, functools.partial(lambda n, i: (0,) * n, a.ndim)) for a in (side, *given)]
        out_shape = (rows, share * part) if given else (share, rows, part)
        return pl.pallas_call(
            kernel,
            grid=(1,),
            out_shape=shape(*out_shape, dtype=BF if given else F32),
            in_specs=full[:1] + [half] * len(pieces) + full[1:],
            out_specs=pl.BlockSpec(out_shape, lambda i: (0,) * len(out_shape)),
            compiler_params=PARAMS,
            cost_estimate=cost(n * hid * (rows + share * part), rows * n * hid * share * part),
        )(side, *pieces, *given)

    def body(tokens, gain, gate_weight, up_weight, down_weight):
        rows, width = tokens.shape
        hid = gate_weight.shape[1]
        share = groups if width // groups % 128 == 0 else 1
        part = width // share
        own = gate_weight.T, up_weight.T
        me = lax.axis_index("gx")
        plane, quad = me // 4, me % 4
        half = lax.axis_index("groups") % 2 if paired else jnp.int32(0)
        turns = jnp.array([[p for _, p in row] + [m for m, _ in row] for row in table], jnp.int32)
        spot = jnp.concatenate([jnp.stack([plane, quad, half]), lax.dynamic_index_in_dim(turns, plane, 0, keepdims=False)])

        values = tokens.astype(F32)
        squares = split(jnp.sum(values * values, axis=1)[None, :])
        lanes = min(rows, width)
        extra = jnp.concatenate([squares[:, i : i + lanes] for i in range(0, rows, lanes)])
        scaled = (values * gain[None, :]).astype(BF)
        blocks = [jnp.concatenate([scaled, jnp.pad(extra, ((0, 0), (0, width - lanes)))])]
        for s in range(1, planes):
            for way in (1, -1):
                blocks.append(lax.ppermute(blocks[0] if s == 1 else blocks[-2], "gx", line(s, way)))
        parts = [b[rows + i : rows + i + EXTRA, :lanes] for b in blocks for i in range(0, len(extra), EXTRA)]
        parts = [jnp.concatenate([joined(p) for p in parts[i :: len(extra) // EXTRA]]) for i in range(len(extra) // EXTRA)]
        total = jnp.concatenate([jnp.sum(p, axis=0, keepdims=True) for p in parts], axis=1)

        def far_cut(i, after):
            return cut(spot, *own, width, (2,) if paired else (2, 3), cuts[i][0], len(cuts[i]), after=after)

        first_sends = far_cut(0, (blocks[0],))

        def first_moves(given, outs):
            _, quad = place()
            g = lax.axis_index("groups") if share > 1 else 0
            moves = []
            for other in range(2):
                for p in range(planes):
                    for y in range(2):
                        target = p * 4 + y * 2 + lax.bitwise_xor(lax.rem(quad, 2), other)
                        columns = pl.ds(pl.multiple_of(target * width + g * part, part), part)
                        moves.append((given[0], (slice(None), columns), outs[other], (y, p)))
            return moves

        keep, send = move(first_moves, [shape(2, planes, hid, part)] * 2, down_weight, after=first_sends)
        came = lax.ppermute(send, "gx", flip(1))

        def second_moves(given, outs):
            _, quad = place()
            return [(given[dc], lax.bitwise_xor(quad // 2, 1), outs[0], dc) for dc in range(2)]

        send = move(second_moves, [shape(2, planes, hid, part)], keep, came, after=(blocks[0],))[0]
        across = lax.ppermute(send, "gx", flip(2))

        far = []
        for i, js in enumerate(cuts):
            sends = far_cut(1, (send, *blocks[3:5])) if i else first_sends
            if paired:
                brought = lax.ppermute(sends[0], ("groups", "gx"), far_flip())
                far.append((brought, lax.ppermute(brought, "groups", [(i, i ^ 1) for i in range(groups)])))
            else:
                far.append(tuple(lax.ppermute(w, "gx", flip(d)) for d, w in zip((2, 3), sends)))
        near = lax.ppermute(cut(spot, *own, width, (1,), 0, planes, after=first_sends)[0], "gx", flip(1))


        def third_moves(ks, given, outs):
            plane, quad = place()
            moves = []
            for i, k in enumerate(ks):
                p = lax.rem(plane + planes - k, planes)
                for dc in range(2):
                    moves.append((given[dc], (quad // 2, p), outs[i], (0, dc)))
                    moves.append((given[2], (dc, p), outs[i], (1, dc)))
            return moves

        ready = move(
            functools.partial(third_moves, range(planes)), [shape(2, 2, hid, part)] * planes, keep, came, across, after=blocks[-4:-2]
        )
        sums = product(spot, rows, blocks, own, near, far[0], cuts[0], after=(across,))
        held = [lax.ppermute(h, "gx", shift(-k)) if k else h for k, h in enumerate(ready)]
        pieces = list(held)
        for r in range(1, share):
            pieces += [lax.ppermute(h, "groups", swap(r)) for h in held]

        crossed = pieces[planes:] if share > 1 else held
        one, two, three = held[1], held[2 % planes], held[-1]
        x0, x1, x2, x3 = crossed[0], crossed[1], crossed[2 % planes], crossed[-1]
        later = [(one, two), (), (three, x2, x1)]
        keep, send = product(spot, rows, blocks, own, near, far[1], cuts[1], sums, total, after=(x0,))
        came = lax.ppermute(send, "gx", flip(1))
        mine, total, send = stage(
            meet, [shape(2 * hid, rows, dtype=F32), shape(1, rows, dtype=F32), shape(EXTRA + 2 * hid, rows)], keep, total, came,
            after=later[0],
        )
        came = lax.ppermute(send, "gx", flip(2))
        hidden = stage(activate, [shape(hid, rows)], mine, total, came, after=later[1])[0]
        beside = [lax.ppermute(hidden, "gx", shift(-k, d)) if k or d else hidden for k in range(planes) for d in (0, 2)]
        beside = move(
            lambda given, outs: [(a, ..., outs[0], (i // 2, i % 2)) for i, a in enumerate(given)],
            [shape(planes, 2, hid, rows)],
            *beside,
            after=later[2],
        )[0]
        other = lax.ppermute(beside, "gx", flip(1))
        return mix(other, pieces, share, 1, mix(beside, pieces, share, 0))

    return body


def solution(mesh):
    body = make_body(mesh.shape["gx"], mesh.shape["groups"])
    in_specs = (P("groups", "gx"), P("gx"), P(None, "gx"), P(None, "gx"), P("gx", None))
    out_specs = P("groups", "gx")
    return jax.shard_map(body, mesh=mesh, in_specs=in_specs, out_specs=out_specs, check_vma=False)
```

```python
import functools

import jax
import jax.numpy as jnp
from jax import lax
from jax.experimental import pallas as pl
from jax.experimental.pallas import tpu as pltpu
from jax.sharding import PartitionSpec as P

D = 16384
BF = jnp.bfloat16
F32 = jnp.float32
ANY = pl.BlockSpec(memory_space=pl.ANY)
VMEM = pl.BlockSpec(memory_space=pltpu.VMEM)
PARAMS = pltpu.CompilerParams(vmem_limit_bytes=48 * 1024 * 1024)
HEAVY = 20
EXTRA = 16


def shape(*dims, dtype=BF):
    return jax.ShapeDtypeStruct(dims, dtype)


def cost(size, flops=0, heavy=HEAVY):
    return pl.CostEstimate(flops=int(heavy * flops), bytes_accessed=int(heavy * size), transcendentals=0)


def move(moves, outs, *operands, after=()):
    def kernel(*refs):
        for source, where, target, there in moves(refs[: len(operands)], refs[len(operands) + len(after) :]):
            target[there] = source[where]

    return pl.pallas_call(
        kernel,
        out_shape=outs,
        in_specs=[VMEM] * len(operands) + [ANY] * len(after),
        out_specs=[VMEM] * len(outs),
        compiler_params=PARAMS,
        cost_estimate=cost(4 * sum(o.size for o in outs), 0, 1),
    )(*operands, *after)


def split(values):
    parts = []
    for _ in range(3):
        parts.append(lax.reduce_precision(values, 8, 7))
        values = values - parts[-1]
    return jnp.pad(jnp.concatenate(parts), ((0, EXTRA - 3), (0, 0))).astype(BF)


def joined(parts):
    parts = parts.astype(F32)
    return parts[0:1] + parts[1:2] + parts[2:3]


def stage(kernel, outs, *operands, after=()):
    def body(*refs):
        kernel(*refs[: len(operands)], *refs[len(operands) + len(after) :])

    return pl.pallas_call(
        body,
        out_shape=outs,
        in_specs=[VMEM] * len(operands) + [ANY] * len(after),
        out_specs=[VMEM] * len(outs),
        compiler_params=PARAMS,
        cost_estimate=cost(4 * sum(o.size for o in outs), 0, 1),
    )(*operands, *after)


def put_parts(values, out):
    parts = []
    for _ in range(3):
        parts.append(values.astype(BF).astype(F32))
        values = values - parts[-1]
    out[pl.ds(0, EXTRA), :] = jnp.concatenate(parts + [jnp.zeros((EXTRA - 3, values.shape[1]), F32)]).astype(BF)


def meet(keep, total, came, mine, total_out, send):
    count = keep.shape[0] // 2
    both = total[...] + joined(came[pl.ds(0, EXTRA), :])
    total_out[...] = both
    mine[...] = keep[pl.ds(0, count), :] + came[pl.ds(EXTRA, count), :].astype(F32)
    put_parts(both, send)
    across = keep[pl.ds(count, count), :] + came[pl.ds(EXTRA + count, count), :].astype(F32)
    send[pl.ds(EXTRA, count), :] = across.astype(BF)


def activate(mine, total, came, hidden):
    hid = hidden.shape[0]
    inverse = lax.rsqrt((total[...] + joined(came[pl.ds(0, EXTRA), :])) / D + 1e-05)
    gate = (mine[pl.ds(0, hid), :] + came[pl.ds(EXTRA, hid), :].astype(F32)) * inverse
    up = (mine[pl.ds(hid, hid), :] + came[pl.ds(EXTRA + hid, hid), :].astype(F32)) * inverse
    hidden[...] = (gate / (1.0 + jnp.exp(-gate)) * up).astype(BF)


def arrivals(planes):
    table = []
    for p in range(planes):
        row = [(0, p)]
        for s in range(1, planes):
            if p >= s:
                row.append((2 * s - 1, p - s))
            if p + s < planes:
                row.append((2 * s, p + s))
        table.append(row)
    return table


def make_body(n, groups):
    planes = n // 4
    table = arrivals(planes)
    BLOCK, ARRAY = 3, 3 + planes
    cuts = [range(0, planes - 1), range(planes - 1, planes)]
    paired = groups % 2 == 0

    def at(p, q):
        return (p % planes) * 4 + q

    def flip(d):
        return [(at(p, q), at(p, q ^ d)) for p in range(planes) for q in range(4)]

    def shift(k, d=0):
        return [(at(p, q), at(p + k, q ^ d)) for p in range(planes) for q in range(4)]

    def line(s, way):
        senders = range(s - 1, planes - 1) if way > 0 else range(1, planes - s + 1)
        return [(at(p, q), at(p + way, q)) for p in senders for q in range(4)]

    def far_flip():
        return [(g * n + i, g * n + j) for g in range(groups) for i, j in flip(2 + g % 2)]

    def swap(r):
        return [((g + r) % groups, g) for g in range(groups)]

    def place():
        me = lax.axis_index("gx")
        return me // 4, me % 4

    def product(spot, rows, blocks, own, near, far, js, total=None, squares=None, after=()):
        width = blocks[0].shape[1]
        _, two, hid, _ = near.shape
        first, count = js[0], len(js)
        lists = [sorted(set(row[j][0] for row in table)) for j in js]
        arrays = sorted(set(sum(lists, [])))
        last = squares is not None
        given = ([] if total is None else [total]) + ([squares] if last else [])

        def kernel(spot, *refs):
            sources, refs = refs[: len(arrays)], refs[len(arrays) :]
            own_gate, own_up, near, far0, far1 = refs[:5]
            if last:
                keep, send, out, xs, sems = refs[-5:]
            else:
                out, xs, sems = refs[-3:]
            i = pl.program_id(0)

            def bring(array, k):
                return pltpu.make_async_copy(sources[arrays.index(array)].at[pl.ds(0, rows)], xs.at[k], sems.at[k])

            @pl.when(i == 0)
            def _():
                for k, choices in enumerate(lists):
                    for array in choices:
                        pl.when(spot[ARRAY + first + k] == array)(bring(array, k).start)
                out[...] = jnp.zeros_like(out) if total is None else refs[5][...]

            for k, choices in enumerate(lists):
                pl.when(i == k)(bring(choices[0], k).wait)

            x = xs[i]
            weights = [own_gate[...], own_up[...]] + [w[0, j] for w in (near, far0, far1) for j in range(2)]
            term = lax.dot_general(
                jnp.concatenate(weights), x, (((1,), (1,)), ((), ())), preferred_element_type=F32
            )
            out[pl.ds(0, 4 * hid), :] += term[: 4 * hid]
            for b in range(2):
                d = 2 + lax.bitwise_xor(b, spot[2])
                out[pl.ds(pl.multiple_of(d * 2 * hid, 8), 2 * hid), :] += term[(4 + 2 * b) * hid : (6 + 2 * b) * hid]
            if last:

                @pl.when(i == count - 1)
                def _():
                    put_parts(refs[4 + len(given)][...], send)
                    for b in range(2):
                        keep[pl.ds(b * 2 * hid, 2 * hid), :] = out[pl.ds(b * 4 * hid, 2 * hid), :]
                        send[pl.ds(EXTRA + b * 2 * hid, 2 * hid), :] = out[pl.ds((4 * b + 2) * hid, 2 * hid), :].astype(BF)

        near_block = pl.BlockSpec((1, two, hid, width), lambda i, spot: (i + first, 0, 0, 0))
        far_block = pl.BlockSpec((1, two, hid, width), lambda i, spot: (i, 0, 0, 0))
        mine = pl.BlockSpec((hid, width), lambda i, spot: (0, spot[BLOCK + first + i] * 4 + spot[1]))

        def whole(*dims):
            return pl.BlockSpec(dims, lambda i, spot: (0, 0))

        scratch = [pltpu.VMEM((count, rows, width), BF), pltpu.SemaphoreType.DMA((count,))]
        if last:
            outs = [shape(4 * hid, rows, dtype=F32), shape(EXTRA + 4 * hid, rows)]
            scratch = [pltpu.VMEM((8 * hid, rows), F32)] + scratch
        else:
            outs = shape(8 * hid, rows, dtype=F32)
        return pl.pallas_call(
            kernel,
            grid_spec=pltpu.PrefetchScalarGridSpec(
                num_scalar_prefetch=1,
                grid=(count,),
                in_specs=[ANY] * len(arrays)
                + [mine, mine, near_block, far_block, far_block]
                + [whole(*g.shape) for g in given]
                + [ANY] * len(after),
                out_specs=[whole(*o.shape) for o in outs] if last else whole(*outs.shape),
                scratch_shapes=scratch,
            ),
            out_shape=outs,
            compiler_params=PARAMS,
            cost_estimate=cost(16 * hid * width * count, 16 * hid * rows * width * count, 1),
        )(spot, *[blocks[m] for m in arrays], *own, near, *far, *given, *after)

    def cut(spot, gate_t, up_t, width, ds, first, count, after=()):
        hid = gate_t.shape[0]

        def kernel(spot, *refs):
            outs = refs[2 * len(ds) + len(after) :]
            for d, out in enumerate(outs):
                for j in range(2):
                    out[0, j] = refs[2 * d + j][...]

        def taken(d):
            def index(s, spot):
                other = lax.bitwise_xor(spot[1], d + spot[2] if d == 2 and paired else d)
                return 0, spot[BLOCK + first + s] * 4 + other

            return pl.BlockSpec((hid, width), index)

        return pl.pallas_call(
            kernel,
            grid_spec=pltpu.PrefetchScalarGridSpec(
                num_scalar_prefetch=1,
                grid=(count,),
                in_specs=[taken(d) for d in ds for _ in range(2)] + [ANY] * len(after),
                out_specs=[pl.BlockSpec((1, 2, hid, width), lambda s, spot: (s, 0, 0, 0))] * len(ds),
            ),
            out_shape=[shape(count, 2, hid, width)] * len(ds),
            compiler_params=PARAMS,
            cost_estimate=cost(8 * len(ds) * count * hid * width, 0, 1),
        )(spot, *[gate_t, up_t] * len(ds), *after)

    def mix(side, pieces, share, dc, total=None):
        rows = side.shape[-1]
        part = pieces[0].shape[-1]
        hid = side.shape[2]
        given = [] if total is None else [total]

        def kernel(side, *refs):
            out = refs[-1]
            g = lax.axis_index("groups")
            left = jnp.concatenate([side[k, dy] for k in range(planes) for dy in range(2)])
            for r in range(share):
                held = refs[r * planes : (r + 1) * planes]
                right = jnp.concatenate([h[dy, 0] for h in held for dy in range(2)])
                sums = lax.dot_general(left, right, (((0,), (0,)), ((), ())), preferred_element_type=F32)
                if not given:
                    out[r] = sums
                    continue
                sums = (refs[-2][r] + sums).astype(BF)
                if share == 1:
                    out[...] = sums
                else:
                    out[:, pl.ds(pl.multiple_of((g + r) % share * part, part), part)] = sums

        half = pl.BlockSpec((2, 1, hid, part), lambda i: (0, dc, 0, 0))
        full = [pl.BlockSpec(a.shape, functools.partial(lambda n, i: (0,) * n, a.ndim)) for a in (side, *given)]
        out_shape = (rows, share * part) if given else (share, rows, part)
        return pl.pallas_call(
            kernel,
            grid=(1,),
            out_shape=shape(*out_shape, dtype=BF if given else F32),
            in_specs=full[:1] + [half] * len(pieces) + full[1:],
            out_specs=pl.BlockSpec(out_shape, lambda i: (0,) * len(out_shape)),
            compiler_params=PARAMS,
            cost_estimate=cost(n * hid * (rows + share * part), rows * n * hid * share * part),
        )(side, *pieces, *given)

    def body(tokens, gain, gate_weight, up_weight, down_weight):
        rows, width = tokens.shape
        hid = gate_weight.shape[1]
        share = groups if width // groups % 128 == 0 else 1
        part = width // share
        own = gate_weight.T, up_weight.T
        me = lax.axis_index("gx")
        plane, quad = me // 4, me % 4
        half = lax.axis_index("groups") % 2 if paired else jnp.int32(0)
        turns = jnp.array([[p for _, p in row] + [m for m, _ in row] for row in table], jnp.int32)
        spot = jnp.concatenate([jnp.stack([plane, quad, half]), lax.dynamic_index_in_dim(turns, plane, 0, keepdims=False)])

        values = tokens.astype(F32)
        squares = split(jnp.sum(values * values, axis=1)[None, :])
        lanes = min(rows, width)
        extra = jnp.concatenate([squares[:, i : i + lanes] for i in range(0, rows, lanes)])
        scaled = (values * gain[None, :]).astype(BF)
        blocks = [jnp.concatenate([scaled, jnp.pad(extra, ((0, 0), (0, width - lanes)))])]
        for s in range(1, planes):
            for way in (1, -1):
                blocks.append(lax.ppermute(blocks[0] if s == 1 else blocks[-2], "gx", line(s, way)))
        parts = [b[rows + i : rows + i + EXTRA, :lanes] for b in blocks for i in range(0, len(extra), EXTRA)]
        parts = [jnp.concatenate([joined(p) for p in parts[i :: len(extra) // EXTRA]]) for i in range(len(extra) // EXTRA)]
        total = jnp.concatenate([jnp.sum(p, axis=0, keepdims=True) for p in parts], axis=1)

        def far_cut(i, after):
            return cut(spot, *own, width, (2,) if paired else (2, 3), cuts[i][0], len(cuts[i]), after=after)

        first_sends = far_cut(0, (blocks[0],))

        def first_moves(given, outs):
            _, quad = place()
            g = lax.axis_index("groups") if share > 1 else 0
            moves = []
            for other in range(2):
                for p in range(planes):
                    for y in range(2):
                        target = p * 4 + y * 2 + lax.bitwise_xor(lax.rem(quad, 2), other)
                        columns = pl.ds(pl.multiple_of(target * width + g * part, part), part)
                        moves.append((given[0], (slice(None), columns), outs[other], (y, p)))
            return moves

        keep, send = move(first_moves, [shape(2, planes, hid, part)] * 2, down_weight, after=first_sends)
        came = lax.ppermute(send, "gx", flip(1))

        def second_moves(given, outs):
            _, quad = place()
            return [(given[dc], lax.bitwise_xor(quad // 2, 1), outs[0], dc) for dc in range(2)]

        send = move(second_moves, [shape(2, planes, hid, part)], keep, came, after=(blocks[0],))[0]
        across = lax.ppermute(send, "gx", flip(2))

        far = []
        for i, js in enumerate(cuts):
            sends = far_cut(1, (send, *blocks[3:5])) if i else first_sends
            if paired:
                brought = lax.ppermute(sends[0], ("groups", "gx"), far_flip())
                far.append((brought, lax.ppermute(brought, "groups", [(i, i ^ 1) for i in range(groups)])))
            else:
                far.append(tuple(lax.ppermute(w, "gx", flip(d)) for d, w in zip((2, 3), sends)))
        near = lax.ppermute(cut(spot, *own, width, (1,), 0, planes, after=first_sends)[0], "gx", flip(1))


        def third_moves(ks, given, outs):
            plane, quad = place()
            moves = []
            for i, k in enumerate(ks):
                p = lax.rem(plane + planes - k, planes)
                for dc in range(2):
                    moves.append((given[dc], (quad // 2, p), outs[i], (0, dc)))
                    moves.append((given[2], (dc, p), outs[i], (1, dc)))
            return moves

        ready = move(
            functools.partial(third_moves, range(planes)), [shape(2, 2, hid, part)] * planes, keep, came, across, after=blocks[-4:-2]
        )
        sums = product(spot, rows, blocks, own, near, far[0], cuts[0], after=(across,))
        held = [lax.ppermute(h, "gx", shift(-k)) if k else h for k, h in enumerate(ready)]
        pieces = list(held)
        for r in range(1, share):
            pieces += [lax.ppermute(h, "groups", swap(r)) for h in held]

        crossed = pieces[planes:] if share > 1 else held
        one, two, three = held[1], held[2 % planes], held[-1]
        x0, x1, x2, x3 = crossed[0], crossed[1], crossed[2 % planes], crossed[-1]
        later = [(two,), (one,), (three, x2, x1)]
        keep, send = product(spot, rows, blocks, own, near, far[1], cuts[1], sums, total, after=(x0,))
        came = lax.ppermute(send, "gx", flip(1))
        mine, total, send = stage(
            meet, [shape(2 * hid, rows, dtype=F32), shape(1, rows, dtype=F32), shape(EXTRA + 2 * hid, rows)], keep, total, came,
            after=later[0],
        )
        came = lax.ppermute(send, "gx", flip(2))
        hidden = stage(activate, [shape(hid, rows)], mine, total, came, after=later[1])[0]
        column = {0: hidden}
        for k in sorted(range(1, planes), key=lambda k: -min(k, planes - k)):
            column[k] = lax.ppermute(hidden, "gx", shift(-k))
        beside = []
        for k in range(planes):
            beside += [column[k], lax.ppermute(column[k], "gx", flip(2))]
        beside = move(
            lambda given, outs: [(a, ..., outs[0], (i // 2, i % 2)) for i, a in enumerate(given)],
            [shape(planes, 2, hid, rows)],
            *beside,
            after=later[2],
        )[0]
        other = lax.ppermute(beside, "gx", flip(1))
        return mix(other, pieces, share, 1, mix(beside, pieces, share, 0))

    return body


def solution(mesh):
    body = make_body(mesh.shape["gx"], mesh.shape["groups"])
    in_specs = (P("groups", "gx"), P("gx"), P(None, "gx"), P(None, "gx"), P("gx", None))
    out_specs = P("groups", "gx")
    return jax.shard_map(body, mesh=mesh, in_specs=in_specs, out_specs=out_specs, check_vma=False)
```

```python
import functools

import jax
import jax.numpy as jnp
from jax import lax
from jax.experimental import pallas as pl
from jax.experimental.pallas import tpu as pltpu
from jax.sharding import PartitionSpec as P

D = 16384
BF = jnp.bfloat16
F32 = jnp.float32
ANY = pl.BlockSpec(memory_space=pl.ANY)
VMEM = pl.BlockSpec(memory_space=pltpu.VMEM)
PARAMS = pltpu.CompilerParams(vmem_limit_bytes=48 * 1024 * 1024)
HEAVY = 20
EXTRA = 16


def shape(*dims, dtype=BF):
    return jax.ShapeDtypeStruct(dims, dtype)


def cost(size, flops=0, heavy=HEAVY):
    return pl.CostEstimate(flops=int(heavy * flops), bytes_accessed=int(heavy * size), transcendentals=0)


def move(moves, outs, *operands, after=()):
    def kernel(*refs):
        for source, where, target, there in moves(refs[: len(operands)], refs[len(operands) + len(after) :]):
            target[there] = source[where]

    return pl.pallas_call(
        kernel,
        out_shape=outs,
        in_specs=[VMEM] * len(operands) + [ANY] * len(after),
        out_specs=[VMEM] * len(outs),
        compiler_params=PARAMS,
        cost_estimate=cost(4 * sum(o.size for o in outs), 0, 20),
    )(*operands, *after)


def split(values):
    parts = []
    for _ in range(3):
        parts.append(lax.reduce_precision(values, 8, 7))
        values = values - parts[-1]
    return jnp.pad(jnp.concatenate(parts), ((0, EXTRA - 3), (0, 0))).astype(BF)


def joined(parts):
    parts = parts.astype(F32)
    return parts[0:1] + parts[1:2] + parts[2:3]


def stage(kernel, outs, *operands, after=()):
    def body(*refs):
        kernel(*refs[: len(operands)], *refs[len(operands) + len(after) :])

    return pl.pallas_call(
        body,
        out_shape=outs,
        in_specs=[VMEM] * len(operands) + [ANY] * len(after),
        out_specs=[VMEM] * len(outs),
        compiler_params=PARAMS,
        cost_estimate=cost(4 * sum(o.size for o in outs), 0, 2),
    )(*operands, *after)


def put_parts(values, out):
    parts = []
    for _ in range(3):
        parts.append(values.astype(BF).astype(F32))
        values = values - parts[-1]
    out[pl.ds(0, EXTRA), :] = jnp.concatenate(parts + [jnp.zeros((EXTRA - 3, values.shape[1]), F32)]).astype(BF)


def meet(keep, total, came, mine, total_out, send):
    count = keep.shape[0] // 2
    both = total[...] + joined(came[pl.ds(0, EXTRA), :])
    total_out[...] = both
    mine[...] = keep[pl.ds(0, count), :] + came[pl.ds(EXTRA, count), :].astype(F32)
    put_parts(both, send)
    across = keep[pl.ds(count, count), :] + came[pl.ds(EXTRA + count, count), :].astype(F32)
    send[pl.ds(EXTRA, count), :] = across.astype(BF)


def activate(mine, total, came, hidden):
    hid = hidden.shape[0]
    inverse = lax.rsqrt((total[...] + joined(came[pl.ds(0, EXTRA), :])) / D + 1e-05)
    gate = (mine[pl.ds(0, hid), :] + came[pl.ds(EXTRA, hid), :].astype(F32)) * inverse
    up = (mine[pl.ds(hid, hid), :] + came[pl.ds(EXTRA + hid, hid), :].astype(F32)) * inverse
    hidden[...] = (gate / (1.0 + jnp.exp(-gate)) * up).astype(BF)


def arrivals(planes):
    table = []
    for p in range(planes):
        row = [(0, p)]
        for s in range(1, planes):
            if p >= s:
                row.append((2 * s - 1, p - s))
            if p + s < planes:
                row.append((2 * s, p + s))
        table.append(row)
    return table


def make_body(n, groups):
    planes = n // 4
    table = arrivals(planes)
    BLOCK, ARRAY = 3, 3 + planes
    cuts = [range(0, planes - 1), range(planes - 1, planes)]
    paired = groups % 2 == 0

    def at(p, q):
        return (p % planes) * 4 + q

    def flip(d):
        return [(at(p, q), at(p, q ^ d)) for p in range(planes) for q in range(4)]

    def shift(k, d=0):
        return [(at(p, q), at(p + k, q ^ d)) for p in range(planes) for q in range(4)]

    def line(s, way):
        senders = range(s - 1, planes - 1) if way > 0 else range(1, planes - s + 1)
        return [(at(p, q), at(p + way, q)) for p in senders for q in range(4)]

    def far_flip():
        return [(g * n + i, g * n + j) for g in range(groups) for i, j in flip(2 + g % 2)]

    def swap(r):
        return [((g + r) % groups, g) for g in range(groups)]

    def place():
        me = lax.axis_index("gx")
        return me // 4, me % 4

    def product(spot, rows, blocks, own, near, far, js, total=None, squares=None, after=()):
        width = blocks[0].shape[1]
        _, two, hid, _ = near.shape
        first, count = js[0], len(js)
        lists = [sorted(set(row[j][0] for row in table)) for j in js]
        arrays = sorted(set(sum(lists, [])))
        last = squares is not None
        given = ([] if total is None else [total]) + ([squares] if last else [])

        def kernel(spot, *refs):
            sources, refs = refs[: len(arrays)], refs[len(arrays) :]
            own_gate, own_up, near, far0, far1 = refs[:5]
            if last:
                keep, send, out, xs, sems = refs[-5:]
            else:
                out, xs, sems = refs[-3:]
            i = pl.program_id(0)

            def bring(array, k):
                return pltpu.make_async_copy(sources[arrays.index(array)].at[pl.ds(0, rows)], xs.at[k], sems.at[k])

            @pl.when(i == 0)
            def _():
                for k, choices in enumerate(lists):
                    for array in choices:
                        pl.when(spot[ARRAY + first + k] == array)(bring(array, k).start)
                out[...] = jnp.zeros_like(out) if total is None else refs[5][...]

            for k, choices in enumerate(lists):
                pl.when(i == k)(bring(choices[0], k).wait)

            x = xs[i]
            weights = [own_gate[...], own_up[...]] + [w[0, j] for w in (near, far0, far1) for j in range(2)]
            term = lax.dot_general(
                jnp.concatenate(weights), x, (((1,), (1,)), ((), ())), preferred_element_type=F32
            )
            out[pl.ds(0, 4 * hid), :] += term[: 4 * hid]
            for b in range(2):
                d = 2 + lax.bitwise_xor(b, spot[2])
                out[pl.ds(pl.multiple_of(d * 2 * hid, 8), 2 * hid), :] += term[(4 + 2 * b) * hid : (6 + 2 * b) * hid]
            if last:

                @pl.when(i == count - 1)
                def _():
                    put_parts(refs[4 + len(given)][...], send)
                    for b in range(2):
                        keep[pl.ds(b * 2 * hid, 2 * hid), :] = out[pl.ds(b * 4 * hid, 2 * hid), :]
                        send[pl.ds(EXTRA + b * 2 * hid, 2 * hid), :] = out[pl.ds((4 * b + 2) * hid, 2 * hid), :].astype(BF)

        near_block = pl.BlockSpec((1, two, hid, width), lambda i, spot: (i + first, 0, 0, 0))
        far_block = pl.BlockSpec((1, two, hid, width), lambda i, spot: (i, 0, 0, 0))
        mine = pl.BlockSpec((hid, width), lambda i, spot: (0, spot[BLOCK + first + i] * 4 + spot[1]))

        def whole(*dims):
            return pl.BlockSpec(dims, lambda i, spot: (0, 0))

        scratch = [pltpu.VMEM((count, rows, width), BF), pltpu.SemaphoreType.DMA((count,))]
        if last:
            outs = [shape(4 * hid, rows, dtype=F32), shape(EXTRA + 4 * hid, rows)]
            scratch = [pltpu.VMEM((8 * hid, rows), F32)] + scratch
        else:
            outs = shape(8 * hid, rows, dtype=F32)
        return pl.pallas_call(
            kernel,
            grid_spec=pltpu.PrefetchScalarGridSpec(
                num_scalar_prefetch=1,
                grid=(count,),
                in_specs=[ANY] * len(arrays)
                + [mine, mine, near_block, far_block, far_block]
                + [whole(*g.shape) for g in given]
                + [ANY] * len(after),
                out_specs=[whole(*o.shape) for o in outs] if last else whole(*outs.shape),
                scratch_shapes=scratch,
            ),
            out_shape=outs,
            compiler_params=PARAMS,
            cost_estimate=cost(16 * hid * width * count, 16 * hid * rows * width * count, 5 if last else 1),
        )(spot, *[blocks[m] for m in arrays], *own, near, *far, *given, *after)

    def cut(spot, gate_t, up_t, width, ds, first, count, after=()):
        hid = gate_t.shape[0]

        def kernel(spot, *refs):
            outs = refs[2 * len(ds) + len(after) :]
            for d, out in enumerate(outs):
                for j in range(2):
                    out[0, j] = refs[2 * d + j][...]

        def taken(d):
            def index(s, spot):
                other = lax.bitwise_xor(spot[1], d + spot[2] if d == 2 and paired else d)
                return 0, spot[BLOCK + first + s] * 4 + other

            return pl.BlockSpec((hid, width), index)

        return pl.pallas_call(
            kernel,
            grid_spec=pltpu.PrefetchScalarGridSpec(
                num_scalar_prefetch=1,
                grid=(count,),
                in_specs=[taken(d) for d in ds for _ in range(2)] + [ANY] * len(after),
                out_specs=[pl.BlockSpec((1, 2, hid, width), lambda s, spot: (s, 0, 0, 0))] * len(ds),
            ),
            out_shape=[shape(count, 2, hid, width)] * len(ds),
            compiler_params=PARAMS,
            cost_estimate=cost(8 * len(ds) * count * hid * width, 0, 5),
        )(spot, *[gate_t, up_t] * len(ds), *after)

    def mix(side, pieces, share, dc, total=None):
        rows = side.shape[-1]
        part = pieces[0].shape[-1]
        hid = side.shape[2]
        given = [] if total is None else [total]

        def kernel(side, *refs):
            out = refs[-1]
            g = lax.axis_index("groups")
            left = jnp.concatenate([side[k, dy] for k in range(planes) for dy in range(2)])
            for r in range(share):
                held = refs[r * planes : (r + 1) * planes]
                right = jnp.concatenate([h[dy, 0] for h in held for dy in range(2)])
                sums = lax.dot_general(left, right, (((0,), (0,)), ((), ())), preferred_element_type=F32)
                if not given:
                    out[r] = sums
                    continue
                sums = (refs[-2][r] + sums).astype(BF)
                if share == 1:
                    out[...] = sums
                else:
                    out[:, pl.ds(pl.multiple_of((g + r) % share * part, part), part)] = sums

        half = pl.BlockSpec((2, 1, hid, part), lambda i: (0, dc, 0, 0))
        full = [pl.BlockSpec(a.shape, functools.partial(lambda n, i: (0,) * n, a.ndim)) for a in (side, *given)]
        out_shape = (rows, share * part) if given else (share, rows, part)
        return pl.pallas_call(
            kernel,
            grid=(1,),
            out_shape=shape(*out_shape, dtype=BF if given else F32),
            in_specs=full[:1] + [half] * len(pieces) + full[1:],
            out_specs=pl.BlockSpec(out_shape, lambda i: (0,) * len(out_shape)),
            compiler_params=PARAMS,
            cost_estimate=cost(n * hid * (rows + share * part), rows * n * hid * share * part),
        )(side, *pieces, *given)

    def body(tokens, gain, gate_weight, up_weight, down_weight):
        rows, width = tokens.shape
        hid = gate_weight.shape[1]
        share = groups if width // groups % 128 == 0 else 1
        part = width // share
        own = gate_weight.T, up_weight.T
        me = lax.axis_index("gx")
        plane, quad = me // 4, me % 4
        half = lax.axis_index("groups") % 2 if paired else jnp.int32(0)
        turns = jnp.array([[p for _, p in row] + [m for m, _ in row] for row in table], jnp.int32)
        spot = jnp.concatenate([jnp.stack([plane, quad, half]), lax.dynamic_index_in_dim(turns, plane, 0, keepdims=False)])

        values = tokens.astype(F32)
        squares = split(jnp.sum(values * values, axis=1)[None, :])
        lanes = min(rows, width)
        extra = jnp.concatenate([squares[:, i : i + lanes] for i in range(0, rows, lanes)])
        scaled = (values * gain[None, :]).astype(BF)
        blocks = [jnp.concatenate([scaled, jnp.pad(extra, ((0, 0), (0, width - lanes)))])]
        for s in range(1, planes):
            for way in (1, -1):
                blocks.append(lax.ppermute(blocks[0] if s == 1 else blocks[-2], "gx", line(s, way)))
        parts = [b[rows + i : rows + i + EXTRA, :lanes] for b in blocks for i in range(0, len(extra), EXTRA)]
        parts = [jnp.concatenate([joined(p) for p in parts[i :: len(extra) // EXTRA]]) for i in range(len(extra) // EXTRA)]
        total = jnp.concatenate([jnp.sum(p, axis=0, keepdims=True) for p in parts], axis=1)

        def far_cut(i, after):
            return cut(spot, *own, width, (2,) if paired else (2, 3), cuts[i][0], len(cuts[i]), after=after)

        first_sends = far_cut(0, (blocks[0],))

        def first_moves(given, outs):
            _, quad = place()
            g = lax.axis_index("groups") if share > 1 else 0
            moves = []
            for other in range(2):
                for p in range(planes):
                    for y in range(2):
                        target = p * 4 + y * 2 + lax.bitwise_xor(lax.rem(quad, 2), other)
                        columns = pl.ds(pl.multiple_of(target * width + g * part, part), part)
                        moves.append((given[0], (slice(None), columns), outs[other], (y, p)))
            return moves

        keep, send = move(first_moves, [shape(2, planes, hid, part)] * 2, down_weight, after=first_sends)
        came = lax.ppermute(send, "gx", flip(1))

        def second_moves(given, outs):
            _, quad = place()
            return [(given[dc], lax.bitwise_xor(quad // 2, 1), outs[0], dc) for dc in range(2)]

        send = move(second_moves, [shape(2, planes, hid, part)], keep, came, after=(blocks[0],))[0]
        across = lax.ppermute(send, "gx", flip(2))

        far = []
        for i, js in enumerate(cuts):
            sends = far_cut(1, (send, *blocks[3:5])) if i else first_sends
            if paired:
                brought = lax.ppermute(sends[0], ("groups", "gx"), far_flip())
                far.append((brought, lax.ppermute(brought, "groups", [(i, i ^ 1) for i in range(groups)])))
            else:
                far.append(tuple(lax.ppermute(w, "gx", flip(d)) for d, w in zip((2, 3), sends)))
        near = lax.ppermute(cut(spot, *own, width, (1,), 0, planes, after=(send,))[0], "gx", flip(1))


        def third_moves(ks, given, outs):
            plane, quad = place()
            moves = []
            for i, k in enumerate(ks):
                p = lax.rem(plane + planes - k, planes)
                for dc in range(2):
                    moves.append((given[dc], (quad // 2, p), outs[i], (0, dc)))
                    moves.append((given[2], (dc, p), outs[i], (1, dc)))
            return moves

        ready = move(
            functools.partial(third_moves, range(planes)), [shape(2, 2, hid, part)] * planes, keep, came, across, after=()
        )
        sums = product(spot, rows, blocks, own, near, far[0], cuts[0], after=(ready[0],))
        held = [lax.ppermute(h, "gx", shift(-k)) if k else h for k, h in enumerate(ready)]
        pieces = list(held)
        for r in range(1, share):
            pieces += [lax.ppermute(h, "groups", swap(r)) for h in held]

        crossed = pieces[planes:] if share > 1 else held
        one, two, three = held[1], held[2 % planes], held[-1]
        x0, x1, x2, x3 = crossed[0], crossed[1], crossed[2 % planes], crossed[-1]
        later = [(), (), (three, x2, x1)]
        keep, send = product(spot, rows, blocks, own, near, far[1], cuts[1], sums, total, after=(x0,))
        came = lax.ppermute(send, "gx", flip(1))
        mine, total, send = stage(
            meet, [shape(2 * hid, rows, dtype=F32), shape(1, rows, dtype=F32), shape(EXTRA + 2 * hid, rows)], keep, total, came,
            after=later[0],
        )
        came = lax.ppermute(send, "gx", flip(2))
        hidden = stage(activate, [shape(hid, rows)], mine, total, came, after=later[1])[0]
        column = {0: hidden}
        for k in sorted(range(1, planes), key=lambda k: -min(k, planes - k)):
            column[k] = lax.ppermute(hidden, "gx", shift(-k))
        beside = []
        for k in range(planes):
            beside += [column[k], lax.ppermute(column[k], "gx", flip(2))]
        beside = move(
            lambda given, outs: [(a, ..., outs[0], (i // 2, i % 2)) for i, a in enumerate(given)],
            [shape(planes, 2, hid, rows)],
            *beside,
            after=later[2],
        )[0]
        other = lax.ppermute(beside, "gx", flip(1))
        return mix(other, pieces, share, 1, mix(beside, pieces, share, 0))

    return body


def solution(mesh):
    body = make_body(mesh.shape["gx"], mesh.shape["groups"])
    in_specs = (P("groups", "gx"), P("gx"), P(None, "gx"), P(None, "gx"), P("gx", None))
    out_specs = P("groups", "gx")
    return jax.shard_map(body, mesh=mesh, in_specs=in_specs, out_specs=out_specs, check_vma=False)
```

```python
import functools

import jax
import jax.numpy as jnp
from jax import lax
from jax.experimental import pallas as pl
from jax.experimental.pallas import tpu as pltpu
from jax.sharding import PartitionSpec as P

D = 16384
BF = jnp.bfloat16
F32 = jnp.float32
ANY = pl.BlockSpec(memory_space=pl.ANY)
VMEM = pl.BlockSpec(memory_space=pltpu.VMEM)
PARAMS = pltpu.CompilerParams(vmem_limit_bytes=48 * 1024 * 1024)
HEAVY = 20
EXTRA = 16


def shape(*dims, dtype=BF):
    return jax.ShapeDtypeStruct(dims, dtype)


def cost(size, flops=0, heavy=HEAVY):
    return pl.CostEstimate(flops=int(heavy * flops), bytes_accessed=int(heavy * size), transcendentals=0)


def move(moves, outs, *operands, after=()):
    def kernel(*refs):
        for source, where, target, there in moves(refs[: len(operands)], refs[len(operands) + len(after) :]):
            target[there] = source[where]

    return pl.pallas_call(
        kernel,
        out_shape=outs,
        in_specs=[VMEM] * len(operands) + [ANY] * len(after),
        out_specs=[VMEM] * len(outs),
        compiler_params=PARAMS,
        cost_estimate=cost(4 * sum(o.size for o in outs), 0, 20),
    )(*operands, *after)


def split(values):
    parts = []
    for _ in range(3):
        parts.append(lax.reduce_precision(values, 8, 7))
        values = values - parts[-1]
    return jnp.pad(jnp.concatenate(parts), ((0, EXTRA - 3), (0, 0))).astype(BF)


def joined(parts):
    parts = parts.astype(F32)
    return parts[0:1] + parts[1:2] + parts[2:3]


def stage(kernel, outs, *operands, after=()):
    def body(*refs):
        kernel(*refs[: len(operands)], *refs[len(operands) + len(after) :])

    return pl.pallas_call(
        body,
        out_shape=outs,
        in_specs=[VMEM] * len(operands) + [ANY] * len(after),
        out_specs=[VMEM] * len(outs),
        compiler_params=PARAMS,
        cost_estimate=cost(4 * sum(o.size for o in outs), 0, 2),
    )(*operands, *after)


def put_parts(values, out):
    parts = []
    for _ in range(3):
        parts.append(values.astype(BF).astype(F32))
        values = values - parts[-1]
    out[pl.ds(0, EXTRA), :] = jnp.concatenate(parts + [jnp.zeros((EXTRA - 3, values.shape[1]), F32)]).astype(BF)


def meet(keep, total, came, mine, total_out, send):
    count = keep.shape[0] // 2
    both = total[...] + joined(came[pl.ds(0, EXTRA), :])
    total_out[...] = both
    mine[...] = keep[pl.ds(0, count), :] + came[pl.ds(EXTRA, count), :].astype(F32)
    put_parts(both, send)
    across = keep[pl.ds(count, count), :] + came[pl.ds(EXTRA + count, count), :].astype(F32)
    send[pl.ds(EXTRA, count), :] = across.astype(BF)


def activate(mine, total, came, hidden):
    hid = hidden.shape[0]
    inverse = lax.rsqrt((total[...] + joined(came[pl.ds(0, EXTRA), :])) / D + 1e-05)
    gate = (mine[pl.ds(0, hid), :] + came[pl.ds(EXTRA, hid), :].astype(F32)) * inverse
    up = (mine[pl.ds(hid, hid), :] + came[pl.ds(EXTRA + hid, hid), :].astype(F32)) * inverse
    hidden[...] = (gate / (1.0 + jnp.exp(-gate)) * up).astype(BF)


def arrivals(planes):
    table = []
    for p in range(planes):
        row = [(0, p)]
        for s in range(1, planes):
            if p >= s:
                row.append((2 * s - 1, p - s))
            if p + s < planes:
                row.append((2 * s, p + s))
        table.append(row)
    return table


def make_body(n, groups):
    planes = n // 4
    table = arrivals(planes)
    BLOCK, ARRAY = 3, 3 + planes
    cuts = [range(0, planes - 1), range(planes - 1, planes)]
    paired = groups % 2 == 0

    def at(p, q):
        return (p % planes) * 4 + q

    def flip(d):
        return [(at(p, q), at(p, q ^ d)) for p in range(planes) for q in range(4)]

    def shift(k, d=0):
        return [(at(p, q), at(p + k, q ^ d)) for p in range(planes) for q in range(4)]

    def line(s, way):
        senders = range(s - 1, planes - 1) if way > 0 else range(1, planes - s + 1)
        return [(at(p, q), at(p + way, q)) for p in senders for q in range(4)]

    def far_flip():
        return [(g * n + i, g * n + j) for g in range(groups) for i, j in flip(2 + g % 2)]

    def swap(r):
        return [((g + r) % groups, g) for g in range(groups)]

    def place():
        me = lax.axis_index("gx")
        return me // 4, me % 4

    def product(spot, rows, blocks, own, near, far, js, total=None, squares=None, after=()):
        width = blocks[0].shape[1]
        _, two, hid, _ = near.shape
        first, count = js[0], len(js)
        lists = [sorted(set(row[j][0] for row in table)) for j in js]
        arrays = sorted(set(sum(lists, [])))
        last = squares is not None
        given = ([] if total is None else [total]) + ([squares] if last else [])

        def kernel(spot, *refs):
            sources, refs = refs[: len(arrays)], refs[len(arrays) :]
            own_gate, own_up, near, far0, far1 = refs[:5]
            if last:
                keep, send, out, xs, sems = refs[-5:]
            else:
                out, xs, sems = refs[-3:]
            i = pl.program_id(0)

            def bring(array, k):
                return pltpu.make_async_copy(sources[arrays.index(array)].at[pl.ds(0, rows)], xs.at[k], sems.at[k])

            @pl.when(i == 0)
            def _():
                for k, choices in enumerate(lists):
                    for array in choices:
                        pl.when(spot[ARRAY + first + k] == array)(bring(array, k).start)
                out[...] = jnp.zeros_like(out) if total is None else refs[5][...]

            for k, choices in enumerate(lists):
                pl.when(i == k)(bring(choices[0], k).wait)

            x = xs[i]
            weights = [own_gate[...], own_up[...]] + [w[0, j] for w in (near, far0, far1) for j in range(2)]
            term = lax.dot_general(
                jnp.concatenate(weights), x, (((1,), (1,)), ((), ())), preferred_element_type=F32
            )
            out[pl.ds(0, 4 * hid), :] += term[: 4 * hid]
            for b in range(2):
                d = 2 + lax.bitwise_xor(b, spot[2])
                out[pl.ds(pl.multiple_of(d * 2 * hid, 8), 2 * hid), :] += term[(4 + 2 * b) * hid : (6 + 2 * b) * hid]
            if last:

                @pl.when(i == count - 1)
                def _():
                    put_parts(refs[4 + len(given)][...], send)
                    for b in range(2):
                        keep[pl.ds(b * 2 * hid, 2 * hid), :] = out[pl.ds(b * 4 * hid, 2 * hid), :]
                        send[pl.ds(EXTRA + b * 2 * hid, 2 * hid), :] = out[pl.ds((4 * b + 2) * hid, 2 * hid), :].astype(BF)

        near_block = pl.BlockSpec((1, two, hid, width), lambda i, spot: (i + first, 0, 0, 0))
        far_block = pl.BlockSpec((1, two, hid, width), lambda i, spot: (i, 0, 0, 0))
        mine = pl.BlockSpec((hid, width), lambda i, spot: (0, spot[BLOCK + first + i] * 4 + spot[1]))

        def whole(*dims):
            return pl.BlockSpec(dims, lambda i, spot: (0, 0))

        scratch = [pltpu.VMEM((count, rows, width), BF), pltpu.SemaphoreType.DMA((count,))]
        if last:
            outs = [shape(4 * hid, rows, dtype=F32), shape(EXTRA + 4 * hid, rows)]
            scratch = [pltpu.VMEM((8 * hid, rows), F32)] + scratch
        else:
            outs = shape(8 * hid, rows, dtype=F32)
        return pl.pallas_call(
            kernel,
            grid_spec=pltpu.PrefetchScalarGridSpec(
                num_scalar_prefetch=1,
                grid=(count,),
                in_specs=[ANY] * len(arrays)
                + [mine, mine, near_block, far_block, far_block]
                + [whole(*g.shape) for g in given]
                + [ANY] * len(after),
                out_specs=[whole(*o.shape) for o in outs] if last else whole(*outs.shape),
                scratch_shapes=scratch,
            ),
            out_shape=outs,
            compiler_params=PARAMS,
            cost_estimate=cost(16 * hid * width * count, 16 * hid * rows * width * count, 5 if last else 1),
        )(spot, *[blocks[m] for m in arrays], *own, near, *far, *given, *after)

    def cut(spot, gate_t, up_t, width, ds, first, count, after=()):
        hid = gate_t.shape[0]

        def kernel(spot, *refs):
            outs = refs[2 * len(ds) + len(after) :]
            for d, out in enumerate(outs):
                for j in range(2):
                    out[0, j] = refs[2 * d + j][...]

        def taken(d):
            def index(s, spot):
                other = lax.bitwise_xor(spot[1], d + spot[2] if d == 2 and paired else d)
                return 0, spot[BLOCK + first + s] * 4 + other

            return pl.BlockSpec((hid, width), index)

        return pl.pallas_call(
            kernel,
            grid_spec=pltpu.PrefetchScalarGridSpec(
                num_scalar_prefetch=1,
                grid=(count,),
                in_specs=[taken(d) for d in ds for _ in range(2)] + [ANY] * len(after),
                out_specs=[pl.BlockSpec((1, 2, hid, width), lambda s, spot: (s, 0, 0, 0))] * len(ds),
            ),
            out_shape=[shape(count, 2, hid, width)] * len(ds),
            compiler_params=PARAMS,
            cost_estimate=cost(8 * len(ds) * count * hid * width, 0, 5),
        )(spot, *[gate_t, up_t] * len(ds), *after)

    def mix(side, pieces, share, dc, total=None):
        rows = side.shape[-1]
        part = pieces[0].shape[-1]
        hid = side.shape[2]
        given = [] if total is None else [total]

        def kernel(side, *refs):
            out = refs[-1]
            g = lax.axis_index("groups")
            left = jnp.concatenate([side[k, dy] for k in range(planes) for dy in range(2)])
            for r in range(share):
                held = refs[r * planes : (r + 1) * planes]
                right = jnp.concatenate([h[dy, 0] for h in held for dy in range(2)])
                sums = lax.dot_general(left, right, (((0,), (0,)), ((), ())), preferred_element_type=F32)
                if not given:
                    out[r] = sums
                    continue
                sums = (refs[-2][r] + sums).astype(BF)
                if share == 1:
                    out[...] = sums
                else:
                    out[:, pl.ds(pl.multiple_of((g + r) % share * part, part), part)] = sums

        half = pl.BlockSpec((2, 1, hid, part), lambda i: (0, dc, 0, 0))
        full = [pl.BlockSpec(a.shape, functools.partial(lambda n, i: (0,) * n, a.ndim)) for a in (side, *given)]
        out_shape = (rows, share * part) if given else (share, rows, part)
        return pl.pallas_call(
            kernel,
            grid=(1,),
            out_shape=shape(*out_shape, dtype=BF if given else F32),
            in_specs=full[:1] + [half] * len(pieces) + full[1:],
            out_specs=pl.BlockSpec(out_shape, lambda i: (0,) * len(out_shape)),
            compiler_params=PARAMS,
            cost_estimate=cost(n * hid * (rows + share * part), rows * n * hid * share * part),
        )(side, *pieces, *given)

    def body(tokens, gain, gate_weight, up_weight, down_weight):
        rows, width = tokens.shape
        hid = gate_weight.shape[1]
        share = groups if width // groups % 128 == 0 else 1
        part = width // share
        own = gate_weight.T, up_weight.T
        me = lax.axis_index("gx")
        plane, quad = me // 4, me % 4
        half = lax.axis_index("groups") % 2 if paired else jnp.int32(0)
        turns = jnp.array([[p for _, p in row] + [m for m, _ in row] for row in table], jnp.int32)
        spot = jnp.concatenate([jnp.stack([plane, quad, half]), lax.dynamic_index_in_dim(turns, plane, 0, keepdims=False)])

        values = tokens.astype(F32)
        squares = split(jnp.sum(values * values, axis=1)[None, :])
        lanes = min(rows, width)
        extra = jnp.concatenate([squares[:, i : i + lanes] for i in range(0, rows, lanes)])
        scaled = (values * gain[None, :]).astype(BF)
        blocks = [jnp.concatenate([scaled, jnp.pad(extra, ((0, 0), (0, width - lanes)))])]
        for s in range(1, planes):
            for way in (1, -1):
                blocks.append(lax.ppermute(blocks[0] if s == 1 else blocks[-2], "gx", line(s, way)))
        parts = [b[rows + i : rows + i + EXTRA, :lanes] for b in blocks for i in range(0, len(extra), EXTRA)]
        parts = [jnp.concatenate([joined(p) for p in parts[i :: len(extra) // EXTRA]]) for i in range(len(extra) // EXTRA)]
        total = jnp.concatenate([jnp.sum(p, axis=0, keepdims=True) for p in parts], axis=1)

        def far_cut(i, after):
            return cut(spot, *own, width, (2,) if paired else (2, 3), cuts[i][0], len(cuts[i]), after=after)

        first_sends = far_cut(0, (blocks[0],))

        def first_moves(given, outs):
            _, quad = place()
            g = lax.axis_index("groups") if share > 1 else 0
            moves = []
            for other in range(2):
                for p in range(planes):
                    for y in range(2):
                        target = p * 4 + y * 2 + lax.bitwise_xor(lax.rem(quad, 2), other)
                        columns = pl.ds(pl.multiple_of(target * width + g * part, part), part)
                        moves.append((given[0], (slice(None), columns), outs[other], (y, p)))
            return moves

        keep, send = move(first_moves, [shape(2, planes, hid, part)] * 2, down_weight, after=first_sends)
        came = lax.ppermute(send, "gx", flip(1))

        def second_moves(given, outs):
            _, quad = place()
            return [(given[dc], lax.bitwise_xor(quad // 2, 1), outs[0], dc) for dc in range(2)]

        send = move(second_moves, [shape(2, planes, hid, part)], keep, came, after=(blocks[0],))[0]
        across = lax.ppermute(send, "gx", flip(2))

        far = []
        for i, js in enumerate(cuts):
            sends = far_cut(1, (send, *blocks[3:5])) if i else first_sends
            if paired:
                brought = lax.ppermute(sends[0], ("groups", "gx"), far_flip())
                far.append((brought, lax.ppermute(brought, "groups", [(i, i ^ 1) for i in range(groups)])))
            else:
                far.append(tuple(lax.ppermute(w, "gx", flip(d)) for d, w in zip((2, 3), sends)))
        near = lax.ppermute(cut(spot, *own, width, (1,), 0, planes, after=(send,))[0], "gx", flip(1))


        def third_moves(ks, given, outs):
            plane, quad = place()
            moves = []
            for i, k in enumerate(ks):
                p = lax.rem(plane + planes - k, planes)
                for dc in range(2):
                    moves.append((given[dc], (quad // 2, p), outs[i], (0, dc)))
                    moves.append((given[2], (dc, p), outs[i], (1, dc)))
            return moves

        ready = move(
            functools.partial(third_moves, range(planes)), [shape(2, 2, hid, part)] * planes, keep, came, across, after=()
        )
        sums = product(spot, rows, blocks, own, near, far[0], cuts[0], after=(across,))
        held = [lax.ppermute(h, "gx", shift(-k)) if k else h for k, h in enumerate(ready)]
        pieces = list(held)
        for r in range(1, share):
            pieces += [lax.ppermute(h, "groups", swap(r)) for h in held]

        crossed = pieces[planes:] if share > 1 else held
        one, two, three = held[1], held[2 % planes], held[-1]
        x0, x1, x2, x3 = crossed[0], crossed[1], crossed[2 % planes], crossed[-1]
        later = [(two,), (x2,), (x1,)]
        keep, send = product(spot, rows, blocks, own, near, far[1], cuts[1], sums, total, after=(x0,))
        came = lax.ppermute(send, "gx", flip(1))
        mine, total, send = stage(
            meet, [shape(2 * hid, rows, dtype=F32), shape(1, rows, dtype=F32), shape(EXTRA + 2 * hid, rows)], keep, total, came,
            after=later[0],
        )
        came = lax.ppermute(send, "gx", flip(2))
        hidden = stage(activate, [shape(hid, rows)], mine, total, came, after=later[1])[0]
        column = {0: hidden}
        for k in sorted(range(1, planes), key=lambda k: -min(k, planes - k)):
            column[k] = lax.ppermute(hidden, "gx", shift(-k))
        beside = []
        for k in range(planes):
            beside += [column[k], lax.ppermute(column[k], "gx", flip(2))]
        beside = move(
            lambda given, outs: [(a, ..., outs[0], (i // 2, i % 2)) for i, a in enumerate(given)],
            [shape(planes, 2, hid, rows)],
            *beside,
            after=later[2],
        )[0]
        other = lax.ppermute(beside, "gx", flip(1))
        return mix(other, pieces, share, 1, mix(beside, pieces, share, 0))

    return body


def solution(mesh):
    body = make_body(mesh.shape["gx"], mesh.shape["groups"])
    in_specs = (P("groups", "gx"), P("gx"), P(None, "gx"), P(None, "gx"), P("gx", None))
    out_specs = P("groups", "gx")
    return jax.shard_map(body, mesh=mesh, in_specs=in_specs, out_specs=out_specs, check_vma=False)
```
